256 devices in a mesh: row: 64 (over x, z, core), col: 4 (over y).
Axes of the slice: x: 4, y: 4, z: 8, core: 2. Of those that a mesh axis runs over, the one named last changes fastest.
Arguments:
- features: bfloat16 [262144, 512], P('row'), may hold values from -6 to 6
- history: bfloat16 [262144, 512], P('row'), may hold values from 0 to 2
- weight_one: bfloat16 [512, 512], P(None, 'col'), may hold values from -0.25 to 0.25
- weight_two: bfloat16 [512, 512], P(None, 'col'), may hold values from -0.25 to 0.25
- bias_one: float32 [512], P('col'), may hold values from -3 to 3
- bias_two: float32 [512], P('col'), may hold values from -3 to 3
- adjacency: bfloat16 [12288, 128, 128], P('row'), may hold values from 0 to 0.071777344
- halo_owner: int32 [64, 96], P('row'), may hold values from -1 to 63, as said below
- halo_block: int32 [64, 96], P('row'), may hold values from 0 to 31, as said below
- tile_target: int32 [64, 192], P('row'), may hold values from 0 to 31
- tile_source: int32 [64, 192], P('row'), may hold values from 0 to 127, as said below
- tile_count: int32 [64], P('row'), may hold values from 80 to 192, as said below
Outputs:
- hidden: bfloat16 [262144, 512], P('row', 'col')
- embedding: bfloat16 [262144, 512], P('row', 'col')
The draws below stay inside these ranges and needn't reach their ends.
Inputs may be any that keep to these rules, and one draw needn't show every extreme that they name: `halo_owner`: used slots come first and are followed only by unused ones (-1); at least half of the 96 slots are used and some partition uses all; no partition names itself; at most 2 used slots of one partition name the same owner, and some partition reaches 2. `halo_block`: used slots of one partition that name the same owner name different blocks. `tile_source`: live tiles name only local blocks or used halo slots. `tile_count`: some partition has all 192 tiles live.
All inputs are finite; a program needn't handle non-finite values.
Results may differ from the reference program's by a relative error of at most 0.0046.
Values may be sent and summed in bfloat16 or wider, within the bound.
A program may use at most 128 MiB of HBM per device.

```python
import jax
import jax.numpy as jnp
from jax import lax

F = 512
H = 512
BLOCK = 128
CAP = 2
NB = 32
HALO = 96
TILES = 192
NODES = 262144
N_ROW = 64


def permute_one(subkey):
    return jax.random.permutation(subkey, N_ROW - 1)


def layout(key):
    seeds = [jax.random.fold_in(key, 7100 + number) for number in range(10)]
    part_ids = jnp.arange(N_ROW, dtype=jnp.int32)
    counts = jax.random.randint(seeds[0], (N_ROW,), (HALO + 1) // 2, HALO + 1)
    fullest = jax.random.randint(seeds[1], (), 0, N_ROW)
    counts = jnp.where(part_ids == fullest, HALO, counts)
    orders = jax.vmap(permute_one)(jax.random.split(seeds[2], N_ROW)).astype(jnp.int32)
    shifts = jax.random.randint(seeds[3], (N_ROW, 1), 0, CAP)
    slot_ids = jnp.arange(HALO, dtype=jnp.int32)[None, :]
    groups = (slot_ids + shifts) // CAP
    members = (slot_ids + shifts) % CAP
    offsets = jnp.take_along_axis(orders, groups, axis=1)
    owners = (part_ids[:, None] + 1 + offsets) % N_ROW
    owners = jnp.where(slot_ids < counts[:, None], owners, -1)
    bases = jax.random.randint(seeds[4], (N_ROW, HALO // CAP + 2), 0, NB)
    strides = jax.random.randint(seeds[5], (N_ROW, HALO // CAP + 2), 1, (NB - 1) // (CAP - 1) + 1)
    blocks = (jnp.take_along_axis(bases, groups, axis=1) + members * jnp.take_along_axis(strides, groups, axis=1)) % NB
    tile_counts = jax.random.randint(seeds[6], (N_ROW,), NB + counts, TILES + 1)
    busiest = jax.random.randint(seeds[7], (), 0, N_ROW)
    tile_counts = jnp.where(part_ids == busiest, TILES, tile_counts)
    tile_ids = jnp.arange(TILES, dtype=jnp.int32)[None, :]
    random_target = jax.random.randint(seeds[8], (N_ROW, TILES), 0, NB)
    random_source = jax.random.randint(seeds[9], (N_ROW, TILES), 0, NB + counts[:, None])
    targets = jnp.where(tile_ids < NB, tile_ids, random_target)
    sources = jnp.where(tile_ids < NB + counts[:, None], tile_ids, random_source)
    return (owners.astype(jnp.int32), blocks.astype(jnp.int32), targets.astype(jnp.int32), sources.astype(jnp.int32), tile_counts.astype(jnp.int32))


def draw_halo_owner(key, part):
    return layout(key)[0]


def draw_halo_block(key, part):
    return layout(key)[1]


def draw_tile_target(key, part):
    return layout(key)[2]


def draw_tile_source(key, part):
    return layout(key)[3]


def draw_tile_count(key, part):
    return layout(key)[4]


def shard_levels(stream_key, dims, shards, least, top_value):
    def one(dim, blocks):
        heights = jax.random.uniform(jax.random.fold_in(jax.random.fold_in(stream_key, 6), dim), (blocks,), jnp.float32, least / len(shards), top_value / len(shards))
        return jnp.repeat(jnp.exp(heights), dims[dim] // blocks).reshape((-1,) + (1,) * (len(dims) - dim - 1))

    loudness = one(*shards[0])
    for cut in shards[1:]:
        loudness = loudness * one(*cut)
    return loudness


def centred(key, dims, width, reach, cuts=(), kind=jnp.bfloat16):
    loudness = shard_levels(key, dims, cuts, -0.22, 0.18) if cuts else 1.0
    result = jax.random.normal(key, dims, jnp.float32) * width * loudness
    return jnp.minimum(jnp.maximum(result, -reach), reach).astype(kind)


def setup_inputs(seed: int = 0) -> dict:
    key_of = jax.random.split(jax.random.key(seed), 13)
    return {
        "features": centred(key_of[0], (NODES, F), 1.0, 6.0, ((0, 64),)),
        "history": jnp.clip(2.0 * jax.random.uniform(key_of[1], (NODES, H), jnp.float32) ** shard_levels(key_of[1], (NODES, H), ((0, 64),), -0.2, 0.2), 0.0, 2.0).astype(jnp.bfloat16),
        "weight_one": centred(key_of[2], (F, H), F ** -0.5, 0.25, ((1, 4),)),
        "weight_two": centred(key_of[3], (H, H), H ** -0.5, 0.25, ((1, 4),)),
        "bias_one": centred(key_of[4], (H,), 0.5, 3.0, ((0, 4),), jnp.float32),
        "bias_two": centred(key_of[5], (H,), 0.5, 3.0, ((0, 4),), jnp.float32),
        "adjacency": jnp.clip(0.071777344 * jax.random.uniform(key_of[6], (N_ROW * TILES, BLOCK, BLOCK), jnp.float32) ** shard_levels(key_of[6], (N_ROW * TILES, BLOCK, BLOCK), ((0, 64),), -0.2, 0.2), 0.0, 0.071777344).astype(jnp.bfloat16),
        "halo_owner": draw_halo_owner(jax.random.fold_in(key_of[12], 71), 0),
        "halo_block": draw_halo_block(jax.random.fold_in(key_of[12], 71), 0),
        "tile_target": draw_tile_target(jax.random.fold_in(key_of[12], 71), 0),
        "tile_source": draw_tile_source(jax.random.fold_in(key_of[12], 71), 0),
        "tile_count": draw_tile_count(jax.random.fold_in(key_of[12], 71), 0),
    }


def aggregate(halo_table, own_table, adjacency, halo_owner, halo_block, tile_target, tile_source, tile_count):
    def partition_sum(part_index):
        owners = halo_owner[part_index]
        in_use = owners >= 0
        halo_index = (jnp.where(in_use, owners, 0) * NB + halo_block[part_index]).astype(jnp.int32)
        halos = halo_table[halo_index]
        mine = lax.dynamic_slice_in_dim(own_table, (part_index * NB).astype(jnp.int32), NB, 0)
        sources = jnp.concatenate([mine, halos], axis=0)
        picked = sources[tile_source[part_index]].astype(jnp.float32)
        tiles = lax.dynamic_slice_in_dim(adjacency, (part_index * TILES).astype(jnp.int32), TILES, 0).astype(jnp.float32)
        products = jnp.einsum("tab,tbw->taw", tiles, picked)
        live_tiles = jnp.arange(TILES, dtype=jnp.int32) < tile_count[part_index]
        products = jnp.where(live_tiles[:, None, None], products, jnp.float32(0.0))
        return jax.ops.segment_sum(products, tile_target[part_index], num_segments=NB)
    summed = lax.map(partition_sum, jnp.arange(N_ROW, dtype=jnp.int32))
    return summed.reshape(N_ROW * NB * BLOCK, -1)


def reference(features, history, weight_one, weight_two, bias_one, bias_two, adjacency, halo_owner, halo_block, tile_target, tile_source, tile_count):
    proj_one = jnp.dot(features, weight_one, preferred_element_type=jnp.float32).astype(jnp.bfloat16)
    table_one = proj_one.reshape(N_ROW * NB, BLOCK, H)
    summed_one = aggregate(table_one, table_one, adjacency, halo_owner, halo_block, tile_target, tile_source, tile_count)
    hidden = jnp.maximum(summed_one + bias_one, 0.0).astype(jnp.bfloat16)
    proj_two = jnp.dot(hidden, weight_two, preferred_element_type=jnp.float32).astype(jnp.bfloat16)
    proj_past = jnp.dot(history, weight_two, preferred_element_type=jnp.float32).astype(jnp.bfloat16)
    summed_two = aggregate(proj_past.reshape(N_ROW * NB, BLOCK, H), proj_two.reshape(N_ROW * NB, BLOCK, H), adjacency, halo_owner, halo_block, tile_target, tile_source, tile_count)
    embedding = (summed_two + bias_two).astype(jnp.bfloat16)
    return (hidden, embedding)
```

```python
import functools

import jax
import jax.numpy as jnp
from jax import lax
from jax.experimental import pallas as pl
from jax.experimental.pallas import tpu as pltpu
from jax.sharding import PartitionSpec as P

BLOCK = 128
NB = 32
TILES = 192
HALO = 96
NX, NZ = 4, 8
GROUPS = 8
NEAR = 10
FAR = 6
NEAR_AT = NB
FAR_AT = NB + GROUPS * NEAR
UNROLL = 8
LIST = TILES + UNROLL
VMEM_LIMIT = 48 * 2**20

NEAR_STEPS = (0, 7, 1, 6, 2)
FAR_STEPS = (5, 3, 4)

SMEM = pl.BlockSpec(memory_space=pltpu.SMEM)
VMEM = pl.BlockSpec(memory_space=pltpu.VMEM)
ANY = pl.BlockSpec(memory_space=pl.ANY)
PARAMS = pltpu.CompilerParams(vmem_limit_bytes=VMEM_LIMIT)


def blocks(count):
    return jax.ShapeDtypeStruct((count, BLOCK, BLOCK), jnp.bfloat16)


def row_of(x, z, k):
    return x * (NZ * 2) + z * 2 + k


def member(x, k, group):
    dx, dk = group // 2, group % 2
    return lax.rem(x + dx, NX), k + dk - 2 * k * dk


def prepare_kernel(ids, owner, block, wanted, place):
    x, z, k = ids[0], ids[1], ids[2]

    @pl.loop(0, 128, unroll=8)
    def _(i):
        wanted[0, i] = 0
        place[0, i] = 0

    @pl.loop(0, 64, unroll=8)
    def _(i):
        wanted[1, i] = 0

    @pl.loop(0, HALO)
    def _(h):
        named = owner[0, h]
        o = jnp.maximum(named, 0)
        live = named >= 0
        nth = jnp.where(live, wanted[1, o], 0)
        wanted[1, o] = jnp.where(live, nth + 1, wanted[1, o])
        at = 2 * o + nth
        wanted[0, at] = jnp.where(live, block[0, h], wanted[0, at])
        ox, oz, ok = o // 16, (o // 2) % 8, o % 2
        group = lax.rem(x - ox + NX, NX) * 2 + (k + ok - 2 * k * ok)
        step = lax.rem(oz - z + NZ, NZ)
        spot = jnp.int32(0)
        for i, s in enumerate(NEAR_STEPS):
            spot = jnp.where(step == s, NEAR_AT + group * NEAR + 2 * i, spot)
        for i, s in enumerate(FAR_STEPS):
            spot = jnp.where(step == s, FAR_AT + group * FAR + 2 * i, spot)
        place[0, h] = spot + nth


def prepare(ids, owner, block):
    return pl.pallas_call(
        prepare_kernel,
        out_shape=(
            jax.ShapeDtypeStruct((2, 128), jnp.int32),
            jax.ShapeDtypeStruct((1, 128), jnp.int32),
        ),
        in_specs=[SMEM] * 3,
        out_specs=(SMEM, SMEM),
        name="prepare",
    )(ids, owner, block)


def sort_kernel(target, source, count, place, lists, counts):
    @pl.loop(0, LIST, unroll=8)
    def _(i):
        for c in range(3):
            lists[c, i] = NB << 16

    for c in range(3):
        counts[0, c] = 0

    @pl.loop(0, TILES)
    def _(t):
        s = source[0, t]
        own = s < NB
        spot = jnp.where(own, s, place[0, jnp.clip(s - NB, 0, HALO - 1)])
        kind = jnp.where(own, 0, jnp.where(spot < FAR_AT, 1, 2))
        base = jnp.where(own, 0, jnp.where(spot < FAR_AT, NEAR_AT, FAR_AT))

        @pl.when(t < count[0])
        def _():
            n = counts[0, kind]
            lists[kind, n] = t | ((spot - base) << 8) | (target[0, t] << 16)
            counts[0, kind] = n + 1


def sort_tiles(target, source, count, place):
    return pl.pallas_call(
        sort_kernel,
        out_shape=(
            jax.ShapeDtypeStruct((3, LIST), jnp.int32),
            jax.ShapeDtypeStruct((1, 4), jnp.int32),
        ),
        in_specs=[SMEM] * 4,
        out_specs=(SMEM, SMEM),
        name="sort_tiles",
    )(target, source, count, place)


def relay_kernel(ids, wanted, up_ref, down_ref, up1, up2, down1, down2):
    x, z, k = ids[0], ids[1], ids[2]
    for table, sign, one, two, slot in (
        (up_ref, 1, up1, up2, 0),
        (down_ref, -1, down1, down2, 1),
    ):
        o = row_of(x, lax.rem(z - 2 * sign + NZ, NZ), k)
        z1 = lax.rem(z + sign + NZ, NZ)
        z2 = lax.rem(z + 2 * sign + NZ, NZ)
        for g in range(GROUPS):
            dx, dk = member(x, k, g)
            for p in range(2):
                one[2 * g + p] = table[wanted[row_of(dx, z1, dk), 2 * o + p]]
            two[g] = table[wanted[row_of(dx, z2, dk), 2 * o + slot]]


def relay(ids, wanted, up, down):
    return pl.pallas_call(
        relay_kernel,
        out_shape=(blocks(16), blocks(8), blocks(16), blocks(8)),
        in_specs=[SMEM, SMEM, VMEM, VMEM],
        out_specs=(VMEM,) * 4,
        compiler_params=PARAMS,
        cost_estimate=pl.CostEstimate(flops=0, bytes_accessed=6 << 20, transcendentals=0),
        name="relay",
    )(ids, wanted, up, down)


def near_kernel(ids, wanted, *refs):
    tables, outs = refs[:5], refs[5:]
    x, z, k = ids[0], ids[1], ids[2]
    for g in range(GROUPS):
        dx, dk = member(x, k, g)
        d = row_of(dx, z, dk)
        for i, s in enumerate(NEAR_STEPS):
            o = row_of(x, lax.rem(z + s, NZ), k)
            for p in range(2):
                outs[g][2 * i + p] = tables[i][wanted[d, 2 * o + p]]


def near(ids, wanted, tables):
    return pl.pallas_call(
        near_kernel,
        out_shape=(blocks(NEAR),) * GROUPS,
        in_specs=[SMEM, SMEM] + [VMEM] * 5,
        out_specs=(VMEM,) * GROUPS,
        compiler_params=PARAMS,
        cost_estimate=pl.CostEstimate(flops=0, bytes_accessed=8 << 20, transcendentals=0),
        name="near",
    )(ids, wanted, *tables)


def far_kernel(up3, down3, up4, down4, *outs):
    for g in range(GROUPS):
        outs[g][0:2] = up3[2 * g : 2 * g + 2]
        outs[g][2:4] = down3[2 * g : 2 * g + 2]
        outs[g][4] = up4[g]
        outs[g][5] = down4[g]


def far(up3, down3, up4, down4):
    return pl.pallas_call(
        far_kernel,
        out_shape=(blocks(FAR),) * GROUPS,
        in_specs=[VMEM] * 4,
        out_specs=(VMEM,) * GROUPS,
        compiler_params=PARAMS,
        cost_estimate=pl.CostEstimate(flops=0, bytes_accessed=3 << 20, transcendentals=0),
        name="far",
    )(up3, down3, up4, down4)


def gather_kernel(kind, parts, first, relu, last, *refs):
    lists, counts, adjacency = refs[:3]
    pieces = refs[3 : 3 + parts]
    rest = refs[3 + parts :]
    if not first:
        before, rest = rest[0], rest[1:]
    if last:
        bias, rest = rest[0], rest[1:]
    out, total, held, sem = rest
    width = held.shape[0] // parts
    copies = [
        pltpu.make_async_copy(piece, held.at[pl.ds(i * width, width)], sem.at[i])
        for i, piece in enumerate(pieces)
    ]
    for copy in copies:
        copy.start()
    if first:
        total[...] = jnp.zeros_like(total)
    else:
        total[0:NB] = before[...]
        total[NB] = jnp.zeros((BLOCK, BLOCK), jnp.float32)
    for copy in copies:
        copy.wait()

    @pl.loop(0, (counts[0, kind] + UNROLL - 1) // UNROLL)
    def _(step):
        entries = [lists[kind, step * UNROLL + i] for i in range(UNROLL)]
        products = [
            jnp.dot(
                adjacency[e & 255],
                held[(e >> 8) & 255],
                preferred_element_type=jnp.float32,
            )
            for e in entries
        ]
        for e, product in zip(entries, products):
            total[e >> 16] += product

    if last:

        @pl.loop(0, NB, unroll=2)
        def _(b):
            value = total[b] + bias[...]
            if relu:
                value = jnp.maximum(value, 0.0)
            out[b] = value.astype(jnp.bfloat16)
    else:
        out[...] = total[0:NB]


def gather(kind, lists, counts, adjacency, pieces, before=None, bias=None, relu=False):
    first, last = before is None, bias is not None
    width = pieces[0].shape[0]
    args = [lists, counts, adjacency, *pieces]
    specs = [SMEM, SMEM, VMEM] + [ANY] * len(pieces)
    if not first:
        args.append(before)
        specs.append(VMEM)
    if last:
        args.append(bias.reshape(1, BLOCK))
        specs.append(VMEM)
    return pl.pallas_call(
        functools.partial(gather_kernel, kind, len(pieces), first, relu, last),
        out_shape=jax.ShapeDtypeStruct(
            (NB, BLOCK, BLOCK), jnp.bfloat16 if last else jnp.float32
        ),
        in_specs=specs,
        out_specs=VMEM,
        scratch_shapes=[
            pltpu.VMEM((NB + 1, BLOCK, BLOCK), jnp.float32),
            pltpu.VMEM((width * len(pieces), BLOCK, BLOCK), jnp.bfloat16),
            pltpu.SemaphoreType.DMA((len(pieces),)),
        ],
        compiler_params=PARAMS,
        cost_estimate=pl.CostEstimate(
            flops=2 * 64 * BLOCK**3, bytes_accessed=24 << 20, transcendentals=0
        ),
        name=("own", "near", "far")[kind] + "_tiles",
    )(*args)


def second_kernel(ids, mine, up, down, across_low, across_high, weight, out):
    y = ids[3]

    def part(shift):
        return weight[pl.ds(pl.multiple_of(lax.rem(y + shift, 4) * BLOCK, BLOCK), BLOCK), :]

    def mul(a, w):
        return jnp.dot(a, w, preferred_element_type=jnp.float32)

    half = across_low.shape[0]
    rows = 512

    @pl.loop(0, 2 * half // rows)
    def _(i):
        here = pl.ds(i * rows, rows)
        total = mul(mine[here, :], part(0)) + mul(up[here, :], part(3)) + mul(down[here, :], part(1))

        @pl.when(i < half // rows)
        def _():
            out[here, :] = (total + mul(across_low[here, :], part(2))).astype(jnp.bfloat16)

        @pl.when(i >= half // rows)
        def _():
            there = pl.ds(i * rows - half, rows)
            out[here, :] = (total + mul(across_high[there, :], part(2))).astype(jnp.bfloat16)


def second(ids, mine, up, down, across_low, across_high, weight):
    return pl.pallas_call(
        second_kernel,
        out_shape=jax.ShapeDtypeStruct(mine.shape, jnp.bfloat16),
        in_specs=[SMEM] + [VMEM] * 6,
        out_specs=VMEM,
        compiler_params=PARAMS,
        cost_estimate=pl.CostEstimate(
            flops=2 * 4096 * 512 * 128, bytes_accessed=6 << 20, transcendentals=0
        ),
        name="second",
    )(ids, mine, up, down, across_low, across_high, weight)


def along_z(step):
    return [
        (row_of(x, z, k), row_of(x, (z + step) % NZ, k))
        for x in range(NX)
        for z in range(NZ)
        for k in range(2)
    ]


def along_slab(group):
    dx, dk = group // 2, group % 2
    return [
        (row_of(x, z, k), row_of((x + dx) % NX, z, k ^ dk))
        for x in range(NX)
        for z in range(NZ)
        for k in range(2)
    ]


def along_y(step):
    return [(y, (y + step) % 4) for y in range(4)]


def project(rows, weight):
    return (
        jnp.dot(rows, weight, preferred_element_type=jnp.float32)
        .astype(jnp.bfloat16)
        .reshape(NB, BLOCK, BLOCK)
    )


def tables_of(table):
    up1 = lax.ppermute(table, "row", along_z(1))
    down1 = lax.ppermute(table, "row", along_z(-1))
    up2 = lax.ppermute(up1, "row", along_z(1))
    down2 = lax.ppermute(down1, "row", along_z(-1))
    return (table, up1, down1, up2, down2)


def spread(pieces):
    return [pieces[0]] + [
        lax.ppermute(pieces[g], "row", along_slab(g)) for g in range(1, GROUPS)
    ]


def halo(ids, wanted, tables):
    one_up, two_up, one_down, two_down = relay(ids, wanted, tables[3], tables[4])
    up3 = lax.ppermute(one_up, "row", along_z(1))
    down3 = lax.ppermute(one_down, "row", along_z(-1))
    up4 = lax.ppermute(two_up, "row", along_z(2))
    down4 = lax.ppermute(two_down, "row", along_z(-2))
    near_pieces = spread(near(ids, wanted, tables))
    far_pieces = spread(far(up3, down3, up4, down4))
    return near_pieces, far_pieces


def local(
    features,
    history,
    weight_one,
    weight_two,
    bias_one,
    bias_two,
    adjacency,
    halo_owner,
    halo_block,
    tile_target,
    tile_source,
    tile_count,
):
    row = lax.axis_index("row")
    ids = jnp.stack([row // 16, (row // 2) % 8, row % 2, lax.axis_index("col")]).astype(jnp.int32)
    table_one = project(features, weight_one)
    tables_one = tables_of(table_one)
    mine, place = prepare(ids, halo_owner, halo_block)
    wanted = lax.all_gather(mine[0:1], "row", axis=0, tiled=True)
    lists, counts = sort_tiles(tile_target, tile_source, tile_count, place)
    table_past = project(history, weight_two)
    own_one = gather(0, lists, counts, adjacency, [table_one])
    near_one, far_one = halo(ids, wanted, tables_one)
    table_past, _ = lax.optimization_barrier((table_past, tables_one[4]))
    tables_past = tables_of(table_past)
    sum_one = gather(1, lists, counts, adjacency, near_one, own_one)
    hidden = gather(2, lists, counts, adjacency, far_one, sum_one, bias_one, True)
    hidden = hidden.reshape(NB * BLOCK, BLOCK)
    half = NB * BLOCK // 2
    up = lax.ppermute(hidden, "col", along_y(1))
    down = lax.ppermute(hidden, "col", along_y(-1))
    across_low = lax.ppermute(up[:half], "col", along_y(1))
    across_high = lax.ppermute(down[half:], "col", along_y(-1))
    table_two = second(ids, hidden, up, down, across_low, across_high, weight_two)
    near_two, far_two = halo(ids, wanted, tables_past)
    own_two = gather(0, lists, counts, adjacency, [table_two.reshape(NB, BLOCK, BLOCK)])
    sum_two = gather(1, lists, counts, adjacency, near_two, own_two)
    embedding = gather(2, lists, counts, adjacency, far_two, sum_two, bias_two)
    return (hidden, embedding.reshape(NB * BLOCK, BLOCK))


def solution(mesh):
    return jax.shard_map(
        local,
        mesh=mesh,
        in_specs=(
            P("row", None),
            P("row", None),
            P(None, "col"),
            P(None, "col"),
            P("col"),
            P("col"),
            P("row", None, None),
            P("row", None),
            P("row", None),
            P("row", None),
            P("row", None),
            P("row"),
        ),
        out_specs=(P("row", "col"), P("row", "col")),
        check_vma=False,
    )
```

```python
import functools

import jax
import jax.numpy as jnp
from jax import lax
from jax.experimental import pallas as pl
from jax.experimental.pallas import tpu as pltpu
from jax.sharding import PartitionSpec as P

BLOCK = 128
NB = 32
TILES = 192
HALO = 96
NX, NZ, NY = 4, 8, 4
GROUPS = 8
SHARE = 16
UNROLL = 8
LIST = TILES + UNROLL
CHUNKS = 4
PER = GROUPS // CHUNKS
MESH = pl.DeviceIdType.MESH

STEPS = (0, 7, 1, 6, 2, 5, 3, 4)

SMEM = pl.BlockSpec(memory_space=pltpu.SMEM)
VMEM = pl.BlockSpec(memory_space=pltpu.VMEM)
ANY = pl.BlockSpec(memory_space=pl.ANY)
PARAMS = pltpu.CompilerParams(vmem_limit_bytes=40 * 2**20)


def row_of(x, z, k):
    return x * (NZ * 2) + z * 2 + k


def member(x, k, group):
    dx, dk = group // 2, group % 2
    return lax.rem(x + dx, NX), k + dk - 2 * k * dk


def prepare_kernel(ids, owner, block, wanted, place):
    x, z, k = ids[0], ids[1], ids[2]

    @pl.loop(0, 128, unroll=8)
    def _(i):
        wanted[0, i] = 0
        place[0, i] = 0

    @pl.loop(0, 64, unroll=8)
    def _(i):
        wanted[1, i] = 0

    @pl.loop(0, HALO)
    def _(h):
        named = owner[0, h]
        o = jnp.maximum(named, 0)
        live = named >= 0
        nth = jnp.where(live, wanted[1, o], 0)
        wanted[1, o] = jnp.where(live, nth + 1, wanted[1, o])
        at = 2 * o + nth
        wanted[0, at] = jnp.where(live, block[0, h], wanted[0, at])
        ox, oz, ok = o // 16, (o // 2) % 8, o % 2
        group = lax.rem(x - ox + NX, NX) * 2 + (k + ok - 2 * k * ok)
        step = lax.rem(oz - z + NZ, NZ)
        spot = jnp.int32(0)
        for i, s in enumerate(STEPS):
            spot = jnp.where(step == s, 2 * i, spot)
        place[0, h] = group * SHARE + spot + nth


def prepare(ids, owner, block):
    return pl.pallas_call(
        prepare_kernel,
        out_shape=(
            jax.ShapeDtypeStruct((8, 128), jnp.int32),
            jax.ShapeDtypeStruct((1, 128), jnp.int32),
        ),
        in_specs=[SMEM] * 3,
        out_specs=(SMEM, SMEM),
        cost_estimate=pl.CostEstimate(flops=0, bytes_accessed=16 << 20, transcendentals=0),
        name="prepare",
    )(ids, owner, block)


def sort_kernel(target, source, count, place, lists, counts, order, keep):
    @pl.loop(0, LIST, unroll=8)
    def _(i):
        for c in range(2):
            lists[c, i] = NB << 16

    @pl.loop(0, TILES, unroll=8)
    def _(i):
        order[0, i] = 0
        keep[0, i] = 0.0

    @pl.loop(0, NB, unroll=8)
    def _(i):
        order[1, i] = 0
        order[2, i] = 0

    counts[0, 0] = 0
    live = count[0]
    counts[0, 1] = live

    @pl.loop(0, live)
    def _(t):
        s = source[0, t]
        b = target[0, t]
        own = s < NB
        spot = jnp.where(own, s, NB + place[0, jnp.clip(s - NB, 0, HALO - 1)])
        entry = t | (spot << 8) | (b << 16)
        lists[1, t] = entry
        n = counts[0, 0]
        lists[0, n] = entry
        counts[0, 0] = n + jnp.where(own, 1, 0)
        order[1, b] = order[1, b] + jnp.where(own, 0, 1)

    n = counts[0, 0]
    lists[0, n] = NB << 16

    def start(b, at):
        many = order[1, b]
        order[2, b] = at
        order[1, b] = jnp.maximum(at + many - 1, 0)
        keep[1, b] = jnp.where(many > 0, 1.0, 0.0)
        return at + many

    lax.fori_loop(0, NB, start, jnp.int32(0))

    @pl.loop(0, NB)
    def _(b):
        order[3, b] = order[2, b]

    @pl.loop(0, live)
    def _(t):
        e = lists[1, t]
        b = e >> 16
        spot = (e >> 8) & 255

        @pl.when(spot >= NB)
        def _():
            at = order[2, b]
            order[0, at] = (e & 255) | ((spot - NB) << 8)
            keep[0, at] = jnp.where(at == order[3, b], 0.0, 1.0)
            order[2, b] = at + 1


def sort_tiles(target, source, count, place):
    return pl.pallas_call(
        sort_kernel,
        out_shape=(
            jax.ShapeDtypeStruct((2, LIST), jnp.int32),
            jax.ShapeDtypeStruct((1, 2), jnp.int32),
            jax.ShapeDtypeStruct((4, TILES), jnp.int32),
            jax.ShapeDtypeStruct((2, TILES), jnp.float32),
        ),
        in_specs=[SMEM] * 4,
        out_specs=(SMEM,) * 4,
        cost_estimate=pl.CostEstimate(flops=0, bytes_accessed=24 << 20, transcendentals=0),
        name="sort_tiles",
    )(target, source, count, place)


def gather_kernel(kind, widths, last, *refs):
    lists, counts, adjacency = refs[:3]
    pieces = refs[3 : 3 + len(widths)]
    rest = refs[3 + len(widths) :]
    if last:
        bias, rest = rest[0], rest[1:]
    out, total, held, sem = rest
    copies, at = [], 0
    for i, (piece, width) in enumerate(zip(pieces, widths)):
        copies.append(
            pltpu.make_async_copy(piece, held.at[pl.ds(at, width)], sem.at[i])
        )
        at += width
    for copy in copies:
        copy.start()
    total[...] = jnp.zeros_like(total)
    for copy in copies:
        copy.wait()

    @pl.loop(0, (counts[0, kind] + UNROLL - 1) // UNROLL)
    def _(step):
        entries = [lists[kind, step * UNROLL + i] for i in range(UNROLL)]
        products = [
            jnp.dot(
                adjacency[e & 255],
                held[(e >> 8) & 255],
                preferred_element_type=jnp.float32,
            )
            for e in entries
        ]
        for e, product in zip(entries, products):
            total[e >> 16] += product

    if last:

        @pl.loop(0, NB, unroll=2)
        def _(b):
            out[b] = (total[b] + bias[...]).astype(jnp.bfloat16)
    else:
        out[...] = total[0:NB]


def gather(kind, lists, counts, adjacency, pieces, bias=None):
    last = bias is not None
    widths = [p.shape[0] for p in pieces]
    args = [lists, counts, adjacency, *pieces]
    specs = [SMEM, SMEM, VMEM] + [ANY] * len(pieces)
    if last:
        args.append(bias.reshape(1, BLOCK))
        specs.append(VMEM)
    return pl.pallas_call(
        functools.partial(gather_kernel, kind, widths, last),
        out_shape=jax.ShapeDtypeStruct(
            (NB, BLOCK, BLOCK), jnp.bfloat16 if last else jnp.float32
        ),
        in_specs=specs,
        out_specs=VMEM,
        scratch_shapes=[
            pltpu.VMEM((NB + 1, BLOCK, BLOCK), jnp.float32),
            pltpu.VMEM((sum(widths), BLOCK, BLOCK), jnp.bfloat16),
            pltpu.SemaphoreType.DMA((len(pieces),)),
        ],
        compiler_params=PARAMS,
        cost_estimate=pl.CostEstimate(
            flops=2 * 64 * BLOCK**3, bytes_accessed=16 << 20, transcendentals=0
        ),
        name=("own", "all")[kind] + "_tiles",
    )(*args)


COPIES = 112


def exchange_kernel(
    mine,
    order,
    keep,
    bias,
    weight,
    table_one,
    up_one,
    down_one,
    table_past,
    own,
    adjacency,
    hidden,
    table_two,
    halo_two,
    wanted_all,
    wanted,
    up_two,
    down_two,
    up_past,
    down_past,
    up_past_two,
    down_past_two,
    relay_out,
    relay_in,
    share,
    halo_one,
    sums,
    near_y,
    far_y,
    send_sem,
    recv_sem,
    local_sem,
):
    row = lax.axis_index("row")
    y = lax.axis_index("col")
    x, z, k = row // 16, lax.rem(row // 2, NZ), lax.rem(row, 2)
    me = x * 2 + k
    used = [0]

    def at_z(step):
        return (row_of(x, lax.rem(z + step + NZ, NZ), k), y)

    def at_slab(group):
        ox, ok = member(x, k, group)
        return (row_of(ox, z, ok), y)

    def at_y(step):
        return (row, lax.rem(y + step + NY, NY))

    peers = [at_z(s) for s in (1, -1, 2, -2)]
    peers += [at_slab(g) for g in range(1, GROUPS)]
    peers += [at_y(s) for s in (1, -1)]

    barrier = pltpu.get_barrier_semaphore()
    for peer in peers:
        pl.semaphore_signal(barrier, inc=1, device_id=peer, device_id_type=MESH)
    pl.semaphore_wait(barrier, len(peers))

    started = []

    def send(src, dst, device):
        i = used[0]
        used[0] += 1
        copy = pltpu.make_async_remote_copy(
            src_ref=src,
            dst_ref=dst,
            send_sem=send_sem.at[i],
            recv_sem=recv_sem.at[i],
            device_id=device,
            device_id_type=MESH,
        )
        copy.start()
        started.append(copy)
        return copy

    asks = [
        send(mine, wanted_all.at[2, me], at_slab(g)) for g in range(1, GROUPS)
    ]
    hop = [
        send(up_one, up_two, at_z(1)),
        send(down_one, down_two, at_z(-1)),
    ]
    wanted_all[2, me] = mine[...]
    for copy in asks:
        copy.wait_recv()
    asks = [
        send(wanted_all.at[2], wanted_all.at[2 - s], at_z(s)) for s in (1, -1, 2, -2)
    ]
    for copy in asks:
        copy.wait_recv()
    to_scalars = pltpu.make_async_copy(wanted_all, wanted, local_sem.at[0])
    to_scalars.start()
    to_scalars.wait()

    def pick(shift, group, step, slot):
        ox, ok = member(x, k, group)
        o = row_of(x, lax.rem(z + step + NZ, NZ), k)
        return wanted[2 + shift, ox * 2 + ok, 0, 2 * o + slot]

    def pack_share(parts):
        @pl.loop(0, GROUPS)
        def _(g):
            for i, table in parts:
                for slot in range(2):
                    share[g * SHARE + 2 * i + slot] = table[pick(0, g, STEPS[i], slot)]

    def send_share(layer, g, start, size, halo):
        place = pl.ds(g * SHARE + start, size)
        return send(share.at[place], halo.at[place], at_slab(g))

    def pack_relay(up, down):
        @pl.loop(0, GROUPS)
        def _(g):
            for side, (table, sign) in enumerate(((up, 1), (down, -1))):
                for slot in range(2):
                    relay_out[side, g * 2 + slot] = table[pick(sign, g, -2 * sign, slot)]
                relay_out[2 + side, g] = table[pick(2 * sign, g, -2 * sign, side)]

    def send_relay(layer, c):
        copies = []
        for side, sign in ((0, 1), (1, -1)):
            near = pl.ds(c * PER * 2, PER * 2)
            far = pl.ds(c * PER, PER)
            copies.append(
                send(relay_out.at[2 + side, far], relay_in.at[layer, 2 + side, far], at_z(2 * sign))
            )
            copies.append(
                send(relay_out.at[side, near], relay_in.at[layer, side, near], at_z(sign))
            )
        return copies

    def pack_far(layer, c):
        for g in range(c * PER, (c + 1) * PER):
            place = g * SHARE
            share[place + 10] = relay_in[layer, 0, 2 * g]
            share[place + 11] = relay_in[layer, 0, 2 * g + 1]
            share[place + 12] = relay_in[layer, 1, 2 * g]
            share[place + 13] = relay_in[layer, 1, 2 * g + 1]
            share[place + 14] = relay_in[layer, 2, g]
            share[place + 15] = relay_in[layer, 3, g]

    def forward_far(layer, relays, halo, between):
        copies = []
        for c in range(CHUNKS):
            for copy in relays[c]:
                copy.wait_recv()
            pack_far(layer, c)
            for g in range(max(1, c * PER), (c + 1) * PER):
                copies.append(send_share(layer, g, 10, 6, halo))
            if c in between:
                between[c]()
        return copies

    pack_share([(0, table_one), (1, up_one), (2, down_one)])
    halo_copies = [send_share(0, g, 0, 6, halo_one) for g in range(1, GROUPS)]
    for copy in hop:
        copy.wait_recv()
    pack_relay(up_two, down_two)
    relays = [send_relay(0, c) for c in range(CHUNKS)]
    pack_share([(3, up_two), (4, down_two)])
    halo_copies += [send_share(0, g, 6, 4, halo_one) for g in range(1, GROUPS)]
    past = []

    def start_past():
        past.append(send(table_past, up_past, at_z(1)))
        past.append(send(table_past, down_past, at_z(-1)))

    halo_copies += forward_far(0, relays, halo_one, {0: start_past})
    kept = pltpu.make_async_copy(
        share.at[pl.ds(0, SHARE)], halo_one.at[pl.ds(0, SHARE)], local_sem.at[1]
    )
    kept.start()
    kept.wait()
    for copy in halo_copies:
        copy.wait_recv()

    def tiles(step, total):
        for i in range(UNROLL):
            e = order[0, step * UNROLL + i]
            product = jnp.dot(
                adjacency[e & 255],
                halo_one[e >> 8],
                preferred_element_type=jnp.float32,
            )
            total = total * keep[0, step * UNROLL + i] + product
            sums[step * UNROLL + i] = total
        return total

    lax.fori_loop(0, TILES // UNROLL, tiles, jnp.zeros((BLOCK, BLOCK), jnp.float32))

    @pl.loop(0, NB)
    def _(b):
        value = own[b] + sums[order[1, b]] * keep[1, b] + bias[...]
        hidden[b] = jnp.maximum(value, 0.0).astype(jnp.bfloat16)

    half = NB // 2
    low, high = pl.ds(0, half), pl.ds(half, half)
    for copy in past:
        copy.wait_recv()
    hop = [
        send(up_past, up_past_two, at_z(1)),
        send(down_past, down_past_two, at_z(-1)),
    ]
    beside = [send(hidden, near_y.at[0], at_y(1)), send(hidden, near_y.at[1], at_y(-1))]

    for copy in halo_copies:
        copy.wait_send()
    pack_share([(0, table_past), (1, up_past), (2, down_past)])
    last_copies = [send_share(1, g, 0, 6, halo_two) for g in range(1, GROUPS)]
    for copies in relays:
        for copy in copies:
            copy.wait_send()
    for copy in hop:
        copy.wait_recv()
    pack_relay(up_past_two, down_past_two)
    relays_two = [send_relay(1, c) for c in range(CHUNKS)]
    for copy in beside:
        copy.wait_recv()
    across = [
        send(near_y.at[0, low], far_y.at[low], at_y(1)),
        send(near_y.at[1, high], far_y.at[high], at_y(-1)),
    ]
    pack_share([(3, up_past_two), (4, down_past_two)])
    last_copies += [send_share(1, g, 6, 4, halo_two) for g in range(1, GROUPS)]
    last_copies += forward_far(1, relays_two, halo_two, {})
    kept = pltpu.make_async_copy(
        share.at[pl.ds(0, SHARE)], halo_two.at[pl.ds(0, SHARE)], local_sem.at[2]
    )
    kept.start()
    for copy in across:
        copy.wait_recv()

    def part(shift):
        return weight[pl.ds(pl.multiple_of(lax.rem(y + shift, NY) * BLOCK, BLOCK), BLOCK), :]

    @pl.loop(0, NB // 4)
    def _(i):
        here = pl.ds(i * 4, 4)
        total = jnp.zeros((4 * BLOCK, BLOCK), jnp.float32)
        for rows, shift in ((hidden, 0), (near_y.at[0], 3), (near_y.at[1], 1), (far_y, 2)):
            total += jnp.dot(
                rows[here].reshape(4 * BLOCK, BLOCK),
                part(shift),
                preferred_element_type=jnp.float32,
            )
        table_two[here] = total.astype(jnp.bfloat16).reshape(4, BLOCK, BLOCK)

    for copy in last_copies:
        copy.wait_recv()
    kept.wait()
    waited = halo_copies + [c for copies in relays for c in copies]
    for copy in started:
        if not any(copy is w for w in waited):
            copy.wait_send()


def exchange(mine, order, keep, bias, weight, table_one, up_one, down_one, table_past, own, adjacency):
    def blocks(*count):
        return pltpu.VMEM((*count, BLOCK, BLOCK), jnp.bfloat16)

    table = jax.ShapeDtypeStruct((NB, BLOCK, BLOCK), jnp.bfloat16)
    return pl.pallas_call(
        exchange_kernel,
        out_shape=(
            table,
            table,
            jax.ShapeDtypeStruct((GROUPS * SHARE, BLOCK, BLOCK), jnp.bfloat16),
        ),
        in_specs=[VMEM, SMEM, SMEM] + [VMEM] * 8,
        out_specs=(VMEM, VMEM, ANY),
        scratch_shapes=[
            pltpu.VMEM((5, GROUPS, 8, 128), jnp.int32),
            pltpu.SMEM((5, GROUPS, 8, 128), jnp.int32),
            *[blocks(NB)] * 6,
            blocks(4, 2 * GROUPS),
            blocks(2, 4, 2 * GROUPS),
            blocks(GROUPS * SHARE),
            blocks(GROUPS * SHARE),
            pltpu.VMEM((TILES, BLOCK, BLOCK), jnp.float32),
            blocks(2, NB),
            blocks(NB),
            pltpu.SemaphoreType.DMA((COPIES,)),
            pltpu.SemaphoreType.DMA((COPIES,)),
            pltpu.SemaphoreType.DMA((3,)),
        ],
        compiler_params=pltpu.CompilerParams(
            vmem_limit_bytes=58 * 2**20, collective_id=0, has_side_effects=True
        ),
        cost_estimate=pl.CostEstimate(
            flops=2 * 256 * BLOCK**3, bytes_accessed=32 << 20, transcendentals=0
        ),
        name="exchange",
    )(mine, order, keep, bias.reshape(1, BLOCK), weight, table_one, up_one, down_one, table_past, own, adjacency)


def along_z(step):
    return [
        (row_of(x, z, k), row_of(x, (z + step) % NZ, k))
        for x in range(NX)
        for z in range(NZ)
        for k in range(2)
    ]


def project(rows, weight):
    return (
        jnp.dot(rows, weight, preferred_element_type=jnp.float32)
        .astype(jnp.bfloat16)
        .reshape(NB, BLOCK, BLOCK)
    )


def local(
    features,
    history,
    weight_one,
    weight_two,
    bias_one,
    bias_two,
    adjacency,
    halo_owner,
    halo_block,
    tile_target,
    tile_source,
    tile_count,
):
    row = lax.axis_index("row")
    ids = jnp.stack([row // 16, (row // 2) % 8, row % 2]).astype(jnp.int32)
    table_one = project(features, weight_one)
    up_one = lax.ppermute(table_one, "row", along_z(1))
    down_one = lax.ppermute(table_one, "row", along_z(-1))
    mine, place = prepare(ids, halo_owner, halo_block)
    lists, counts, order, keep = sort_tiles(tile_target, tile_source, tile_count, place)
    table_past = project(history, weight_two)
    own = gather(0, lists, counts, adjacency, [table_one])
    hidden, table_two, halo_two = exchange(
        mine, order, keep, bias_one, weight_two, table_one, up_one, down_one, table_past, own, adjacency
    )
    embedding = gather(1, lists, counts, adjacency, [table_two, halo_two], bias_two)
    return (
        hidden.reshape(NB * BLOCK, BLOCK),
        embedding.reshape(NB * BLOCK, BLOCK),
    )


def solution(mesh):
    return jax.shard_map(
        local,
        mesh=mesh,
        in_specs=(
            P("row", None),
            P("row", None),
            P(None, "col"),
            P(None, "col"),
            P("col"),
            P("col"),
            P("row", None, None),
            P("row", None),
            P("row", None),
            P("row", None),
            P("row", None),
            P("row"),
        ),
        out_specs=(P("row", "col"), P("row", "col")),
        check_vma=False,
    )
```

```python
import jax
import jax.numpy as jnp
from jax import lax
from jax.experimental import pallas as pl
from jax.experimental.pallas import tpu as pltpu
from jax.sharding import PartitionSpec as P

BLOCK = 128
NB = 32
TILES = 192
HALO = 96
NX, NZ, NY = 4, 8, 4
GROUPS = 8
SHARE = 16
UNROLL = 8
FIRSTS = (4, 2, 6, 0)
MESH = pl.DeviceIdType.MESH

STEPS = (0, 7, 1, 6, 2, 5, 3, 4)

SMEM = pl.BlockSpec(memory_space=pltpu.SMEM)
VMEM = pl.BlockSpec(memory_space=pltpu.VMEM)
ANY = pl.BlockSpec(memory_space=pl.ANY)


def row_of(x, z, k):
    return x * (NZ * 2) + z * 2 + k


def member(x, k, group):
    dx, dk = group // 2, group % 2
    return lax.rem(x + dx, NX), k + dk - 2 * k * dk


def prepare_kernel(ids, owner, block, wanted, place):
    x, z, k = ids[0], ids[1], ids[2]

    @pl.loop(0, 128, unroll=8)
    def _(i):
        wanted[0, i] = 0
        place[0, i] = 0

    @pl.loop(0, 64, unroll=8)
    def _(i):
        wanted[1, i] = 0

    @pl.loop(0, HALO)
    def _(h):
        named = owner[0, h]
        o = jnp.maximum(named, 0)
        live = named >= 0
        nth = jnp.where(live, wanted[1, o], 0)
        wanted[1, o] = jnp.where(live, nth + 1, wanted[1, o])
        at = 2 * o + nth
        wanted[0, at] = jnp.where(live, block[0, h], wanted[0, at])
        ox, oz, ok = o // 16, (o // 2) % 8, o % 2
        group = lax.rem(x - ox + NX, NX) * 2 + (k + ok - 2 * k * ok)
        step = lax.rem(oz - z + NZ, NZ)
        spot = jnp.int32(0)
        for i, s in enumerate(STEPS):
            spot = jnp.where(step == s, 2 * i, spot)
        place[0, h] = group * SHARE + spot + nth


def prepare(ids, owner, block):
    return pl.pallas_call(
        prepare_kernel,
        out_shape=(
            jax.ShapeDtypeStruct((8, 128), jnp.int32),
            jax.ShapeDtypeStruct((1, 128), jnp.int32),
        ),
        in_specs=[SMEM] * 3,
        out_specs=(SMEM, SMEM),
        cost_estimate=pl.CostEstimate(flops=0, bytes_accessed=16 << 20, transcendentals=0),
        name="prepare",
    )(ids, owner, block)


def sort_kernel(target, source, count, place, order, keep):
    live = count[0]

    @pl.loop(0, TILES, unroll=8)
    def _(i):
        keep[0, i] = 1.0

    @pl.loop(0, NB + 1, unroll=11)
    def _(b):
        order[2, b] = 0

    @pl.loop(0, TILES, unroll=8)
    def _(t):
        b = jnp.where(t < live, target[0, t], NB)
        order[2, b] = order[2, b] + 1

    def start(b, at):
        many = order[2, b]
        order[2, b] = at
        order[1, b] = jnp.maximum(at + many - 1, 0)
        keep[1, b] = jnp.where(many > 0, 1.0, 0.0)
        first = jnp.minimum(at, TILES - 1)
        keep[0, first] = jnp.where(many > 0, 0.0, keep[0, first])
        return at + many

    lax.fori_loop(0, NB + 1, start, jnp.int32(0))

    @pl.loop(0, TILES, unroll=8)
    def _(t):
        b = jnp.where(t < live, target[0, t], NB)
        s = source[0, t]
        halo = NB + place[0, jnp.clip(s - NB, 0, HALO - 1)]
        at = order[2, b]
        order[0, at] = t | (jnp.where(s < NB, s, halo) << 8)
        order[2, b] = at + 1


def sort_tiles(target, source, count, place):
    return pl.pallas_call(
        sort_kernel,
        out_shape=(
            jax.ShapeDtypeStruct((3, TILES), jnp.int32),
            jax.ShapeDtypeStruct((2, TILES), jnp.float32),
        ),
        in_specs=[SMEM] * 4,
        out_specs=(SMEM,) * 2,
        cost_estimate=pl.CostEstimate(flops=0, bytes_accessed=24 << 20, transcendentals=0),
        name="sort_tiles",
    )(target, source, count, place)


COPIES = 128


def exchange_kernel(
    mine,
    order,
    keep,
    bias_one,
    bias_two,
    weight,
    table_one,
    up_one,
    down_one,
    table_past,
    adjacency_at,
    hidden,
    embedding,
    wanted_all,
    wanted,
    up_two,
    down_two,
    up_past,
    down_past,
    up_past_two,
    down_past_two,
    relay_out,
    relay_in,
    share,
    sources_one,
    sources_two,
    adjacency,
    sums,
    near_y,
    far_y,
    send_sem,
    recv_sem,
    local_sem,
):
    row = lax.axis_index("row")
    y = lax.axis_index("col")
    x, z, k = row // 16, lax.rem(row // 2, NZ), lax.rem(row, 2)
    me = x * 2 + k
    used = [0]

    def at_z(step):
        return (row_of(x, lax.rem(z + step + NZ, NZ), k), y)

    def at_slab(group):
        ox, ok = member(x, k, group)
        return (row_of(ox, z, ok), y)

    def at_y(step):
        return (row, lax.rem(y + step + NY, NY))

    peers = [at_z(s) for s in (1, -1, 2, -2)]
    peers += [at_slab(g) for g in range(1, GROUPS)]
    peers += [at_y(s) for s in (1, -1)]

    barrier = pltpu.get_barrier_semaphore()
    for peer in peers:
        pl.semaphore_signal(barrier, inc=1, device_id=peer, device_id_type=MESH)
    pl.semaphore_wait(barrier, len(peers))

    started = []

    def send(src, dst, device):
        i = used[0]
        used[0] += 1
        copy = pltpu.make_async_remote_copy(
            src_ref=src,
            dst_ref=dst,
            send_sem=send_sem.at[i],
            recv_sem=recv_sem.at[i],
            device_id=device,
            device_id_type=MESH,
        )
        copy.start()
        started.append(copy)
        return copy

    def arrived(copies):
        for copy in copies:
            copy.wait_recv()

    def piece(i, count):
        return pl.ds(i * (NB // count), NB // count)

    asks = [send(mine, wanted_all.at[2, me], at_slab(g)) for g in range(1, GROUPS)]
    hop = [
        [send(up_one.at[p], up_two.at[p], at_z(1)), send(down_one.at[p], down_two.at[p], at_z(-1))]
        for p in (piece(0, 2), piece(1, 2))
    ]
    to_near = pltpu.make_async_copy(adjacency_at, adjacency, local_sem.at[0])
    to_near.start()
    to_sources = pltpu.make_async_copy(table_one, sources_one.at[pl.ds(0, NB)], local_sem.at[1])
    to_sources.start()
    wanted_all[2, me] = mine[...]
    arrived(asks)
    asks = [send(wanted_all.at[2], wanted_all.at[2 - s], at_z(s)) for s in (1, -1, 2, -2)]
    arrived(asks)
    to_scalars = pltpu.make_async_copy(wanted_all, wanted, local_sem.at[2])
    to_scalars.start()
    to_scalars.wait()

    def pick(shift, group, step, slot):
        ox, ok = member(x, k, group)
        o = row_of(x, lax.rem(z + step + NZ, NZ), k)
        return wanted[2 + shift, ox * 2 + ok, 0, 2 * o + slot]

    def pack_share(parts):
        @pl.loop(0, GROUPS)
        def _(g):
            for i, table in parts:
                for slot in range(2):
                    share[g * SHARE + 2 * i + slot] = table[pick(0, g, STEPS[i], slot)]

    def send_share(g, start, size, sources):
        at = g * SHARE + start
        return send(share.at[pl.ds(at, size)], sources.at[pl.ds(NB + at, size)], at_slab(g))

    def pack_relay(up, down):
        @pl.loop(0, GROUPS)
        def _(g):
            for side, (table, sign) in enumerate(((up, 1), (down, -1))):
                for slot in range(2):
                    relay_out[side, g * 2 + slot] = table[pick(sign, g, -2 * sign, slot)]
                relay_out[2 + side, g] = table[pick(2 * sign, g, -2 * sign, side)]

    def send_relay(layer, first):
        near, far = pl.ds(first * 2, 4), pl.ds(first, 2)
        copies = []
        for side, sign in ((0, 1), (1, -1)):
            copies.append(send(relay_out.at[2 + side, far], relay_in.at[layer, 2 + side, far], at_z(2 * sign)))
            copies.append(send(relay_out.at[side, near], relay_in.at[layer, side, near], at_z(sign)))
        return copies

    def pack_far(layer, g):
        at = g * SHARE
        share[at + 10] = relay_in[layer, 0, 2 * g]
        share[at + 11] = relay_in[layer, 0, 2 * g + 1]
        share[at + 12] = relay_in[layer, 1, 2 * g]
        share[at + 13] = relay_in[layer, 1, 2 * g + 1]
        share[at + 14] = relay_in[layer, 2, g]
        share[at + 15] = relay_in[layer, 3, g]

    def forward_far(layer, relays, sources, between):
        copies = []
        for first, then in zip(FIRSTS, between):
            arrived(relays[first])
            for g in (first, first + 1):
                pack_far(layer, g)
                if g > 0:
                    copies.append(send_share(g, 10, 6, sources))
            then()
        return copies

    def keep_own(sources, i):
        copy = pltpu.make_async_copy(
            share.at[pl.ds(0, SHARE)], sources.at[pl.ds(NB, SHARE)], local_sem.at[i]
        )
        copy.start()
        copy.wait()

    def multiply(sources):
        def some(step, total):
            for i in range(UNROLL):
                e = order[0, step * UNROLL + i]
                product = jnp.dot(
                    adjacency[e & 255],
                    sources[e >> 8],
                    preferred_element_type=jnp.float32,
                )
                total = total * keep[0, step * UNROLL + i] + product
                sums[step * UNROLL + i] = total
            return total

        lax.fori_loop(0, TILES // UNROLL, some, jnp.zeros((BLOCK, BLOCK), jnp.float32))

    def summed(b):
        return sums[order[1, b]] * keep[1, b]

    others = range(1, GROUPS)

    pack_share([(0, table_one), (1, up_one), (2, down_one)])
    halo_copies = [send_share(g, 0, 6, sources_one) for g in others]
    past = []

    def start_past():
        p = piece(len(past), 4)
        past.append(
            [send(table_past.at[p], up_past.at[p], at_z(1)), send(table_past.at[p], down_past.at[p], at_z(-1))]
        )

    arrived(hop[0])
    start_past()
    arrived(hop[1])
    pack_relay(up_two, down_two)
    relays = {first: send_relay(0, first) for first in FIRSTS}
    pack_share([(3, up_two), (4, down_two)])
    halo_copies += [send_share(g, 6, 4, sources_one) for g in others]

    def start_two():
        start_past()
        start_past()

    halo_copies += forward_far(
        0, relays, sources_one, (lambda: None, start_past, start_two, lambda: None)
    )
    hop = []
    for i in range(4):
        p = piece(i, 4)
        arrived(past[i])
        hop.append(
            [send(up_past.at[p], up_past_two.at[p], at_z(1)), send(down_past.at[p], down_past_two.at[p], at_z(-1))]
        )
    keep_own(sources_one, 3)
    arrived(halo_copies)
    to_near.wait()
    to_sources.wait()
    multiply(sources_one)

    @pl.loop(0, NB)
    def _(b):
        hidden[b] = jnp.maximum(summed(b) + bias_one[...], 0.0).astype(jnp.bfloat16)

    low, high = piece(0, 2), piece(1, 2)
    from_below = [send(hidden.at[low], near_y.at[0, low], at_y(1))]
    from_above = [send(hidden.at[high], near_y.at[1, high], at_y(-1))]
    from_below.append(send(hidden.at[high], near_y.at[0, high], at_y(1)))
    from_above.append(send(hidden.at[low], near_y.at[1, low], at_y(-1)))

    for copy in halo_copies:
        copy.wait_send()
    pack_share([(0, table_past), (1, up_past), (2, down_past)])
    last_copies = [send_share(g, 0, 6, sources_two) for g in others]
    for copies in relays.values():
        for copy in copies:
            copy.wait_send()
    arrived([from_below[0], from_above[0]])
    across = [
        send(near_y.at[0, low], far_y.at[low], at_y(1)),
        send(near_y.at[1, high], far_y.at[high], at_y(-1)),
    ]
    for copies in hop:
        arrived(copies)
    pack_relay(up_past_two, down_past_two)
    relays_two = {first: send_relay(1, first) for first in FIRSTS}
    pack_share([(3, up_past_two), (4, down_past_two)])
    last_copies += [send_share(g, 6, 4, sources_two) for g in others]
    arrived([from_below[1], from_above[1], *across])

    def part(shift):
        return weight[pl.ds(pl.multiple_of(lax.rem(y + shift, NY) * BLOCK, BLOCK), BLOCK), :]

    @pl.loop(0, NB // 4)
    def _(i):
        here = pl.ds(i * 4, 4)
        total = jnp.zeros((4 * BLOCK, BLOCK), jnp.float32)
        for rows, shift in ((hidden, 0), (near_y.at[0], 3), (near_y.at[1], 1), (far_y, 2)):
            total += jnp.dot(
                rows[here].reshape(4 * BLOCK, BLOCK),
                part(shift),
                preferred_element_type=jnp.float32,
            )
        sources_two[here] = total.astype(jnp.bfloat16).reshape(4, BLOCK, BLOCK)

    last_copies += forward_far(1, relays_two, sources_two, (lambda: None,) * 4)
    keep_own(sources_two, 4)
    arrived(last_copies)
    multiply(sources_two)

    @pl.loop(0, NB)
    def _(b):
        embedding[b] = (summed(b) + bias_two[...]).astype(jnp.bfloat16)

    waited = halo_copies + [c for copies in relays.values() for c in copies]
    for copy in started:
        if not any(copy is w for w in waited):
            copy.wait_send()


def exchange(mine, order, keep, bias_one, bias_two, weight, table_one, up_one, down_one, table_past, adjacency):
    def blocks(*count):
        return pltpu.VMEM((*count, BLOCK, BLOCK), jnp.bfloat16)

    table = jax.ShapeDtypeStruct((NB, BLOCK, BLOCK), jnp.bfloat16)
    return pl.pallas_call(
        exchange_kernel,
        out_shape=(table, table),
        in_specs=[VMEM, SMEM, SMEM] + [VMEM] * 7 + [ANY],
        out_specs=(VMEM, VMEM),
        scratch_shapes=[
            pltpu.VMEM((5, GROUPS, 8, 128), jnp.int32),
            pltpu.SMEM((5, GROUPS, 8, 128), jnp.int32),
            *[blocks(NB)] * 6,
            blocks(4, 2 * GROUPS),
            blocks(2, 4, 2 * GROUPS),
            blocks(GROUPS * SHARE),
            blocks(NB + GROUPS * SHARE),
            blocks(NB + GROUPS * SHARE),
            blocks(TILES),
            pltpu.VMEM((TILES, BLOCK, BLOCK), jnp.float32),
            blocks(2, NB),
            blocks(NB),
            pltpu.SemaphoreType.DMA((COPIES,)),
            pltpu.SemaphoreType.DMA((COPIES,)),
            pltpu.SemaphoreType.DMA((5,)),
        ],
        compiler_params=pltpu.CompilerParams(
            vmem_limit_bytes=60 * 2**20, collective_id=0, has_side_effects=True
        ),
        cost_estimate=pl.CostEstimate(
            flops=2 * 512 * BLOCK**3, bytes_accessed=32 << 20, transcendentals=0
        ),
        name="exchange",
    )(
        mine,
        order,
        keep,
        bias_one.reshape(1, BLOCK),
        bias_two.reshape(1, BLOCK),
        weight,
        table_one,
        up_one,
        down_one,
        table_past,
        adjacency,
    )


def along_z(step):
    return [
        (row_of(x, z, k), row_of(x, (z + step) % NZ, k))
        for x in range(NX)
        for z in range(NZ)
        for k in range(2)
    ]


def project(rows, weight):
    return (
        jnp.dot(rows, weight, preferred_element_type=jnp.float32)
        .astype(jnp.bfloat16)
        .reshape(NB, BLOCK, BLOCK)
    )


def local(
    features,
    history,
    weight_one,
    weight_two,
    bias_one,
    bias_two,
    adjacency,
    halo_owner,
    halo_block,
    tile_target,
    tile_source,
    tile_count,
):
    row = lax.axis_index("row")
    ids = jnp.stack([row // 16, (row // 2) % 8, row % 2]).astype(jnp.int32)
    table_one = project(features, weight_one)
    up_one = lax.ppermute(table_one, "row", along_z(1))
    down_one = lax.ppermute(table_one, "row", along_z(-1))
    mine, place = prepare(ids, halo_owner, halo_block)
    order, keep = sort_tiles(tile_target, tile_source, tile_count, place)
    table_past = project(history, weight_two)
    hidden, embedding = exchange(
        mine, order, keep, bias_one, bias_two, weight_two, table_one, up_one, down_one, table_past, adjacency
    )
    return (
        hidden.reshape(NB * BLOCK, BLOCK),
        embedding.reshape(NB * BLOCK, BLOCK),
    )


def solution(mesh):
    return jax.shard_map(
        local,
        mesh=mesh,
        in_specs=(
            P("row", None),
            P("row", None),
            P(None, "col"),
            P(None, "col"),
            P("col"),
            P("col"),
            P("row", None, None),
            P("row", None),
            P("row", None),
            P("row", None),
            P("row", None),
            P("row"),
        ),
        out_specs=(P("row", "col"), P("row", "col")),
        check_vma=False,
    )
```

```python
import jax
import jax.numpy as jnp
from jax import lax
from jax.experimental import pallas as pl
from jax.experimental.pallas import tpu as pltpu
from jax.sharding import PartitionSpec as P

BLOCK = 128
NB = 32
TILES = 192
HALO = 96
NX, NZ, NY = 4, 8, 4
GROUPS = 8
SHARE = 16
UNROLL = 8
FIRSTS = (4, 2, 6, 0)
MESH = pl.DeviceIdType.MESH

STEPS = (0, 7, 1, 6, 2, 5, 3, 4)

SMEM = pl.BlockSpec(memory_space=pltpu.SMEM)
VMEM = pl.BlockSpec(memory_space=pltpu.VMEM)
ANY = pl.BlockSpec(memory_space=pl.ANY)


def row_of(x, z, k):
    return x * (NZ * 2) + z * 2 + k


def member(x, k, group):
    dx, dk = group // 2, group % 2
    return lax.rem(x + dx, NX), k + dk - 2 * k * dk


def lane(shape, axis):
    return lax.broadcasted_iota(jnp.int32, shape, axis)


def upright(row):
    n = row.shape[1]
    shape = (n, n)
    diagonal = lane(shape, 0) == lane(shape, 1)
    return jnp.sum(jnp.where(diagonal, row, 0), axis=1, keepdims=True)


def request(x, z, k, owner, block, mine):
    row = owner[...]
    named = upright(row)
    square = (HALO, HALO)
    earlier = lane(square, 1) < lane(square, 0)
    nth = jnp.sum(jnp.where((row == named) & earlier, 1, 0), axis=1, keepdims=True)
    code = jnp.where(named >= 0, 2 * named + nth, -1)
    slots = lane((HALO, 128), 1)
    wanted = jnp.sum(jnp.where(code == slots, upright(block[...]), 0), axis=0, keepdims=True)
    mine[...] = jnp.broadcast_to(wanted, (8, 128))
    o = jnp.maximum(named, 0)
    ox, oz, ok = o >> 4, (o >> 1) & 7, o & 1
    group = ((x - ox) & 3) * 2 + (k + ok - 2 * k * ok)
    step = (oz - z) & 7
    spot = jnp.zeros_like(o)
    for i, s in enumerate(STEPS):
        spot = jnp.where(step == s, 2 * i, spot)
    return group * SHARE + spot + jnp.minimum(nth, 1)


def sort(live, target, source, place, listed, kept):
    line, square = (1, TILES), (TILES, TILES)
    ids = lane(line, 1)
    s = source[...]
    slots = lane((HALO, TILES), 0)
    halo = jnp.sum(jnp.where(slots == s - NB, place, 0), axis=0, keepdims=True)
    at = jnp.where(s < NB, s, halo + NB)
    entry = upright(ids + 256 * at)
    row = jnp.where(ids < live, target[...], NB)
    goal = upright(row)
    key = row * 256 + ids
    rank = jnp.sum(jnp.where(key < upright(key), 1, 0), axis=1, keepdims=True)
    here = rank == lane(square, 1)
    order = jnp.sum(jnp.where(here, entry, 0), axis=0, keepdims=True)
    goals = jnp.sum(jnp.where(here, goal, 0), axis=0, keepdims=True)
    before = jnp.sum(jnp.where(goal < goals, 1, 0), axis=0, keepdims=True)
    listed[0:1, 0:TILES] = order
    kept[0:1, 0:TILES] = jnp.where(before == ids, 0.0, 1.0)
    blocks = lane((TILES, 128), 1)
    upto = jnp.sum(jnp.where(goal <= blocks, 1, 0), axis=0, keepdims=True)
    many = jnp.sum(jnp.where(goal == blocks, 1, 0), axis=0, keepdims=True)
    listed[1:2, 0:128] = jnp.maximum(upto - 1, 0)
    kept[1:2, 0:128] = jnp.where(many > 0, 1.0, 0.0)


COPIES = 128


def exchange_kernel(
    count,
    owner,
    block,
    target,
    source,
    bias_one,
    bias_two,
    first_weight,
    weight,
    features,
    history,
    adjacency_at,
    hidden,
    embedding,
    mine,
    listed,
    kept,
    order,
    keep,
    wanted_all,
    wanted,
    stage,
    table_one,
    table_past,
    up_one,
    down_one,
    up_two,
    down_two,
    up_past,
    down_past,
    up_past_two,
    down_past_two,
    relay_out,
    relay_in,
    share,
    sources_one,
    sources_two,
    adjacency,
    sums,
    near_y,
    far_y,
    send_sem,
    recv_sem,
    local_sem,
):
    row = lax.axis_index("row")
    y = lax.axis_index("col")
    x, z, k = row // 16, lax.rem(row // 2, NZ), lax.rem(row, 2)
    me = x * 2 + k
    used = [0]

    def at_z(step):
        return (row_of(x, lax.rem(z + step + NZ, NZ), k), y)

    def at_slab(group):
        ox, ok = member(x, k, group)
        return (row_of(ox, z, ok), y)

    def at_y(step):
        return (row, lax.rem(y + step + NY, NY))

    peers = [at_z(s) for s in (1, -1, 2, -2)]
    peers += [at_slab(g) for g in range(1, GROUPS)]
    peers += [at_y(s) for s in (1, -1)]

    barrier = pltpu.get_barrier_semaphore()
    for peer in peers:
        pl.semaphore_signal(barrier, inc=1, device_id=peer, device_id_type=MESH)

    rows = NB * BLOCK // 4
    pieces = [(table, w, at, i) for table, w, at in ((table_one, first_weight, features), (table_past, weight, history)) for i in range(4)]
    fetches = [
        pltpu.make_async_copy(at.at[pl.ds(i * rows, rows)], stage.at[n % 2], local_sem.at[5 + n])
        for n, (_, _, at, i) in enumerate(pieces)
    ]

    def project(n):
        table, w, _, i = pieces[n]
        fetches[n].wait()

        @pl.loop(0, NB // 8)
        def _(j):
            part = stage[n % 2, pl.ds(j * 2 * BLOCK, 2 * BLOCK)]
            product = jnp.dot(part, w[...], preferred_element_type=jnp.float32)
            table[pl.ds(i * (NB // 4) + 2 * j, 2)] = product.astype(jnp.bfloat16).reshape(2, BLOCK, BLOCK)

        if n + 2 < len(pieces):
            fetches[n + 2].start()

    fetches[0].start()
    fetches[1].start()
    to_near = pltpu.make_async_copy(adjacency_at, adjacency, local_sem.at[0])
    to_near.start()
    place = request(x, z, k, owner, block, mine)
    project(0)
    pl.semaphore_wait(barrier, len(peers))

    started = []

    def send(src, dst, device):
        i = used[0]
        used[0] += 1
        copy = pltpu.make_async_remote_copy(
            src_ref=src,
            dst_ref=dst,
            send_sem=send_sem.at[i],
            recv_sem=recv_sem.at[i],
            device_id=device,
            device_id_type=MESH,
        )
        copy.start()
        started.append(copy)
        return copy

    def arrived(copies):
        for copy in copies:
            copy.wait_recv()

    def piece(i, count):
        return pl.ds(i * (NB // count), NB // count)

    def along_both(up_from, down_from, up_to, down_to, p):
        return [send(up_from.at[p], up_to.at[p], at_z(1)), send(down_from.at[p], down_to.at[p], at_z(-1))]

    quarters = [piece(i, 4) for i in range(4)]
    hop = [along_both(table_one, table_one, up_one, down_one, quarters[0])]
    asks = [send(mine, wanted_all.at[2, me], at_slab(g)) for g in range(1, GROUPS)]
    wanted_all[2, me] = mine[...]
    for i in range(1, 4):
        project(i)
        hop.append(along_both(table_one, table_one, up_one, down_one, quarters[i]))
    to_sources = pltpu.make_async_copy(table_one, sources_one.at[pl.ds(0, NB)], local_sem.at[1])
    to_sources.start()
    arrived(asks)
    asks = [send(wanted_all.at[2], wanted_all.at[2 - s], at_z(s)) for s in (1, -1, 2, -2)]
    sort(count[0], target, source, place, listed, kept)
    to_order = pltpu.make_async_copy(listed, order, local_sem.at[13])
    to_order.start()
    to_keep = pltpu.make_async_copy(kept, keep, local_sem.at[14])
    to_keep.start()
    for i in range(4):
        project(4 + i)
    next_hop = []
    for i in range(2):
        arrived(hop[i])
        next_hop.append(along_both(up_one, down_one, up_two, down_two, quarters[i]))
    arrived(asks)
    to_scalars = pltpu.make_async_copy(wanted_all, wanted, local_sem.at[2])
    to_scalars.start()
    to_scalars.wait()
    to_order.wait()
    to_keep.wait()
    for i in range(2, 4):
        arrived(hop[i])
        next_hop.append(along_both(up_one, down_one, up_two, down_two, quarters[i]))

    def pick(shift, group, step, slot):
        ox, ok = member(x, k, group)
        o = row_of(x, lax.rem(z + step + NZ, NZ), k)
        return jnp.clip(wanted[2 + shift, ox * 2 + ok, 0, 2 * o + slot], 0, NB - 1)

    def pack_share(parts):
        @pl.loop(0, GROUPS)
        def _(g):
            for i, table in parts:
                for slot in range(2):
                    share[g * SHARE + 2 * i + slot] = table[pick(0, g, STEPS[i], slot)]

    def send_share(g, start, size, sources):
        at = g * SHARE + start
        return send(share.at[pl.ds(at, size)], sources.at[pl.ds(NB + at, size)], at_slab(g))

    def pack_relay(up, down):
        @pl.loop(0, GROUPS)
        def _(g):
            for side, (table, sign) in enumerate(((up, 1), (down, -1))):
                for slot in range(2):
                    relay_out[side, g * 2 + slot] = table[pick(sign, g, -2 * sign, slot)]
                relay_out[2 + side, g] = table[pick(2 * sign, g, -2 * sign, side)]

    def send_relay(layer, first):
        near, far = pl.ds(first * 2, 4), pl.ds(first, 2)
        copies = []
        for side, sign in ((0, 1), (1, -1)):
            copies.append(send(relay_out.at[2 + side, far], relay_in.at[layer, 2 + side, far], at_z(2 * sign)))
            copies.append(send(relay_out.at[side, near], relay_in.at[layer, side, near], at_z(sign)))
        return copies

    def pack_far(layer, g):
        at = g * SHARE
        share[at + 10] = relay_in[layer, 0, 2 * g]
        share[at + 11] = relay_in[layer, 0, 2 * g + 1]
        share[at + 12] = relay_in[layer, 1, 2 * g]
        share[at + 13] = relay_in[layer, 1, 2 * g + 1]
        share[at + 14] = relay_in[layer, 2, g]
        share[at + 15] = relay_in[layer, 3, g]

    def forward_far(layer, relays, sources, between):
        copies = []
        for first, then in zip(FIRSTS, between):
            arrived(relays[first])
            for g in (first, first + 1):
                pack_far(layer, g)
                if g > 0:
                    copies.append(send_share(g, 10, 6, sources))
            then()
        return copies

    def keep_own(sources, i):
        copy = pltpu.make_async_copy(
            share.at[pl.ds(0, SHARE)], sources.at[pl.ds(NB, SHARE)], local_sem.at[i]
        )
        copy.start()
        copy.wait()

    def multiply(sources):
        def some(step, total):
            for i in range(UNROLL):
                e = order[0, step * UNROLL + i]
                product = jnp.dot(
                    adjacency[jnp.clip(e & 255, 0, TILES - 1)],
                    sources[jnp.clip(e >> 8, 0, NB + GROUPS * SHARE - 1)],
                    preferred_element_type=jnp.float32,
                )
                total = total * keep[0, step * UNROLL + i] + product
                sums[step * UNROLL + i] = total
            return total

        lax.fori_loop(0, TILES // UNROLL, some, jnp.zeros((BLOCK, BLOCK), jnp.float32))

    def summed(b):
        return sums[jnp.clip(order[1, b], 0, TILES - 1)] * keep[1, b]

    def nothing():
        pass

    others = range(1, GROUPS)

    pack_share([(0, table_one), (1, up_one), (2, down_one)])
    halo_copies = [send_share(g, 0, 6, sources_one) for g in others]
    past = []

    def start_past():
        past.append(along_both(table_past, table_past, up_past, down_past, quarters[len(past)]))

    for i in range(3):
        arrived(next_hop[i])
    start_past()
    arrived(next_hop[3])
    pack_relay(up_two, down_two)
    relays = {first: send_relay(0, first) for first in FIRSTS}
    pack_share([(3, up_two), (4, down_two)])
    halo_copies += [send_share(g, 6, 4, sources_one) for g in others]

    def start_two():
        start_past()
        start_past()

    halo_copies += forward_far(
        0, relays, sources_one, (nothing, start_past, start_two, nothing)
    )
    hop = []
    for i in range(4):
        arrived(past[i])
        hop.append(along_both(up_past, down_past, up_past_two, down_past_two, quarters[i]))
    keep_own(sources_one, 3)
    arrived(halo_copies)
    for copy in halo_copies:
        copy.wait_send()
    pack_share([(0, table_past), (1, up_past), (2, down_past)])
    last_copies = [send_share(g, 0, 6, sources_two) for g in others]
    to_near.wait()
    to_sources.wait()
    multiply(sources_one)

    @pl.loop(0, NB)
    def _(b):
        hidden[b] = jnp.maximum(summed(b) + bias_one[...], 0.0).astype(jnp.bfloat16)

    low, high = piece(0, 2), piece(1, 2)
    from_below = [send(hidden.at[low], near_y.at[0, low], at_y(1))]
    from_above = [send(hidden.at[high], near_y.at[1, high], at_y(-1))]
    from_below.append(send(hidden.at[high], near_y.at[0, high], at_y(1)))
    from_above.append(send(hidden.at[low], near_y.at[1, low], at_y(-1)))

    for copies in relays.values():
        for copy in copies:
            copy.wait_send()
    for copies in hop:
        arrived(copies)
    pack_relay(up_past_two, down_past_two)
    relays_two = {first: send_relay(1, first) for first in FIRSTS}
    pack_share([(3, up_past_two), (4, down_past_two)])
    last_copies += [send_share(g, 6, 4, sources_two) for g in others]
    arrived([from_below[0], from_above[0]])
    across = [
        send(near_y.at[0, low], far_y.at[low], at_y(1)),
        send(near_y.at[1, high], far_y.at[high], at_y(-1)),
    ]

    def part(shift):
        return weight[pl.ds(pl.multiple_of(lax.rem(y + shift, NY) * BLOCK, BLOCK), BLOCK), :]

    def project_hidden():
        arrived([from_below[1], from_above[1], *across])

        @pl.loop(0, NB // 4)
        def _(i):
            here = pl.ds(i * 4, 4)
            total = jnp.zeros((4 * BLOCK, BLOCK), jnp.float32)
            for rows, shift in ((hidden, 0), (near_y.at[0], 3), (near_y.at[1], 1), (far_y, 2)):
                total += jnp.dot(
                    rows[here].reshape(4 * BLOCK, BLOCK),
                    part(shift),
                    preferred_element_type=jnp.float32,
                )
            sources_two[here] = total.astype(jnp.bfloat16).reshape(4, BLOCK, BLOCK)

    last_copies += forward_far(1, relays_two, sources_two, (nothing, nothing, project_hidden, nothing))
    keep_own(sources_two, 4)
    arrived(last_copies)
    multiply(sources_two)

    @pl.loop(0, NB)
    def _(b):
        embedding[b] = (summed(b) + bias_two[...]).astype(jnp.bfloat16)

    waited = halo_copies + [c for copies in relays.values() for c in copies]
    for copy in started:
        if not any(copy is w for w in waited):
            copy.wait_send()


def exchange(count, owner, block, target, source, bias_one, bias_two, weight_one, weight_two, features, history, adjacency):
    def blocks(*count):
        return pltpu.VMEM((*count, BLOCK, BLOCK), jnp.bfloat16)

    table = jax.ShapeDtypeStruct((NB, BLOCK, BLOCK), jnp.bfloat16)
    return pl.pallas_call(
        exchange_kernel,
        out_shape=(table, table),
        in_specs=[SMEM] + [VMEM] * 8 + [ANY] * 3,
        out_specs=(VMEM, VMEM),
        scratch_shapes=[
            pltpu.VMEM((8, 128), jnp.int32),
            pltpu.VMEM((8, 256), jnp.int32),
            pltpu.VMEM((8, 256), jnp.float32),
            pltpu.SMEM((8, 256), jnp.int32),
            pltpu.SMEM((8, 256), jnp.float32),
            pltpu.VMEM((5, GROUPS, 8, 128), jnp.int32),
            pltpu.SMEM((5, GROUPS, 8, 128), jnp.int32),
            pltpu.VMEM((2, NB * BLOCK // 4, 4 * BLOCK), jnp.bfloat16),
            *[blocks(NB)] * 10,
            blocks(4, 2 * GROUPS),
            blocks(2, 4, 2 * GROUPS),
            blocks(GROUPS * SHARE),
            blocks(NB + GROUPS * SHARE),
            blocks(NB + GROUPS * SHARE),
            blocks(TILES),
            pltpu.VMEM((TILES, BLOCK, BLOCK), jnp.float32),
            blocks(2, NB),
            blocks(NB),
            pltpu.SemaphoreType.DMA((COPIES,)),
            pltpu.SemaphoreType.DMA((COPIES,)),
            pltpu.SemaphoreType.DMA((16,)),
        ],
        compiler_params=pltpu.CompilerParams(
            vmem_limit_bytes=60 * 2**20, collective_id=0, has_side_effects=True
        ),
        cost_estimate=pl.CostEstimate(
            flops=2 * 1024 * BLOCK**3, bytes_accessed=32 << 20, transcendentals=0
        ),
        name="exchange",
    )(
        count,
        owner,
        block,
        target,
        source,
        bias_one.reshape(1, BLOCK),
        bias_two.reshape(1, BLOCK),
        weight_one,
        weight_two,
        features,
        history,
        adjacency,
    )


def local(
    features,
    history,
    weight_one,
    weight_two,
    bias_one,
    bias_two,
    adjacency,
    halo_owner,
    halo_block,
    tile_target,
    tile_source,
    tile_count,
):
    hidden, embedding = exchange(
        tile_count,
        halo_owner,
        halo_block,
        tile_target,
        tile_source,
        bias_one,
        bias_two,
        weight_one,
        weight_two,
        features,
        history,
        adjacency,
    )
    return (
        hidden.reshape(NB * BLOCK, BLOCK),
        embedding.reshape(NB * BLOCK, BLOCK),
    )


def solution(mesh):
    return jax.shard_map(
        local,
        mesh=mesh,
        in_specs=(
            P("row", None),
            P("row", None),
            P(None, "col"),
            P(None, "col"),
            P("col"),
            P("col"),
            P("row", None, None),
            P("row", None),
            P("row", None),
            P("row", None),
            P("row", None),
            P("row"),
        ),
        out_specs=(P("row", "col"), P("row", "col")),
        check_vma=False,
    )
```

```python
import jax
import jax.numpy as jnp
from jax import lax
from jax.experimental import pallas as pl
from jax.experimental.pallas import tpu as pltpu
from jax.sharding import PartitionSpec as P

BLOCK = 128
NB = 32
TILES = 192
HALO = 96
NX, NZ, NY = 4, 8, 4
GROUPS = 8
SHARE = 16
UNROLL = 8
FIRSTS = (4, 2, 6, 0)
MESH = pl.DeviceIdType.MESH

STEPS = (0, 7, 1, 6, 2, 5, 3, 4)

SMEM = pl.BlockSpec(memory_space=pltpu.SMEM)
VMEM = pl.BlockSpec(memory_space=pltpu.VMEM)
ANY = pl.BlockSpec(memory_space=pl.ANY)


def row_of(x, z, k):
    return x * (NZ * 2) + z * 2 + k


def member(x, k, group):
    dx, dk = group // 2, group % 2
    return lax.rem(x + dx, NX), k + dk - 2 * k * dk


def lane(shape, axis):
    return lax.broadcasted_iota(jnp.int32, shape, axis)


def upright(row):
    n = row.shape[1]
    shape = (n, n)
    diagonal = lane(shape, 0) == lane(shape, 1)
    return jnp.sum(jnp.where(diagonal, row, 0), axis=1, keepdims=True)


def request(x, z, k, owner, block, mine):
    row = owner[...]
    named = upright(row)
    square = (HALO, HALO)
    earlier = lane(square, 1) < lane(square, 0)
    nth = jnp.sum(jnp.where((row == named) & earlier, 1, 0), axis=1, keepdims=True)
    code = jnp.where(named >= 0, 2 * named + nth, -1)
    slots = lane((HALO, 128), 1)
    wanted = jnp.sum(jnp.where(code == slots, upright(block[...]), 0), axis=0, keepdims=True)
    mine[...] = jnp.broadcast_to(wanted, (8, 128))
    o = jnp.maximum(named, 0)
    ox, oz, ok = o >> 4, (o >> 1) & 7, o & 1
    group = ((x - ox) & 3) * 2 + (k + ok - 2 * k * ok)
    step = (oz - z) & 7
    spot = jnp.zeros_like(o)
    for i, s in enumerate(STEPS):
        spot = jnp.where(step == s, 2 * i, spot)
    return group * SHARE + spot + jnp.minimum(nth, 1)


def sort(live, target, source, place, listed, kept):
    line, square = (1, TILES), (TILES, TILES)
    ids = lane(line, 1)
    s = source[...]
    slots = lane((HALO, TILES), 0)
    halo = jnp.sum(jnp.where(slots == s - NB, place, 0), axis=0, keepdims=True)
    at = jnp.where(s < NB, s, halo + NB)
    entry = upright(ids + 256 * at)
    row = jnp.where(ids < live, target[...], NB)
    goal = upright(row)
    key = row * 256 + ids
    rank = jnp.sum(jnp.where(key < upright(key), 1, 0), axis=1, keepdims=True)
    here = rank == lane(square, 1)
    order = jnp.sum(jnp.where(here, entry, 0), axis=0, keepdims=True)
    goals = jnp.sum(jnp.where(here, goal, 0), axis=0, keepdims=True)
    before = jnp.sum(jnp.where(goal < goals, 1, 0), axis=0, keepdims=True)
    listed[0:1, 0:TILES] = order
    kept[0:1, 0:TILES] = jnp.where(before == ids, 0.0, 1.0)
    blocks = lane((TILES, 128), 1)
    upto = jnp.sum(jnp.where(goal <= blocks, 1, 0), axis=0, keepdims=True)
    many = jnp.sum(jnp.where(goal == blocks, 1, 0), axis=0, keepdims=True)
    listed[1:2, 0:128] = jnp.maximum(upto - 1, 0)
    kept[1:2, 0:128] = jnp.where(many > 0, 1.0, 0.0)


COPIES = 106


def exchange_kernel(
    count,
    owner_at,
    block_at,
    target_at,
    source_at,
    bias_at,
    first_weight_at,
    weight_at,
    features,
    history,
    adjacency_at,
    hidden_at,
    embedding_at,
    owner,
    block,
    target,
    source,
    bias_one,
    first_weight,
    weight,
    hidden,
    embedding,
    mine,
    listed,
    kept,
    order,
    keep,
    wanted_all,
    wanted,
    stage,
    table_one,
    table_past,
    up_one,
    down_one,
    up_two,
    down_two,
    up_past,
    down_past,
    up_past_two,
    down_past_two,
    relay_out,
    relay_in,
    share,
    sources_one,
    sources_two,
    adjacency,
    sums,
    near_y,
    far_y,
    send_sem,
    recv_sem,
    local_sem,
):
    row = lax.axis_index("row")
    y = lax.axis_index("col")
    x, z, k = row // 16, lax.rem(row // 2, NZ), lax.rem(row, 2)
    me = x * 2 + k
    used = [0]

    def at_z(step):
        return (row_of(x, lax.rem(z + step + NZ, NZ), k), y)

    def at_slab(group):
        ox, ok = member(x, k, group)
        return (row_of(ox, z, ok), y)

    def at_y(step):
        return (row, lax.rem(y + step + NY, NY))

    peers = [at_z(s) for s in (1, -1, 2, -2)]
    peers += [at_slab(g) for g in range(1, GROUPS)]
    peers += [at_y(s) for s in (1, -1)]

    barrier = pltpu.get_barrier_semaphore()
    for peer in peers:
        pl.semaphore_signal(barrier, inc=1, device_id=peer, device_id_type=MESH)

    small = [
        pltpu.make_async_copy(at, here, local_sem.at[16 + i])
        for i, (at, here) in enumerate(
            (
                (first_weight_at, first_weight),
                (owner_at, owner),
                (block_at, block),
                (target_at, target),
                (source_at, source),
                (bias_at, bias_one),
                (weight_at, weight),
            )
        )
    ]
    for copy in small[:3]:
        copy.start()

    rows = NB * BLOCK // 4
    pieces = [(table, w, at, i) for table, w, at in ((table_one, first_weight, features), (table_past, weight, history)) for i in range(4)]
    fetches = [
        pltpu.make_async_copy(at.at[pl.ds(i * rows, rows)], stage.at[n % 2], local_sem.at[5 + n])
        for n, (_, _, at, i) in enumerate(pieces)
    ]

    def project(n):
        table, w, _, i = pieces[n]
        fetches[n].wait()

        @pl.loop(0, NB // 8)
        def _(j):
            part = stage[n % 2, pl.ds(j * 2 * BLOCK, 2 * BLOCK)]
            product = jnp.dot(part, w[...], preferred_element_type=jnp.float32)
            table[pl.ds(i * (NB // 4) + 2 * j, 2)] = product.astype(jnp.bfloat16).reshape(2, BLOCK, BLOCK)

        if n + 2 < len(pieces):
            fetches[n + 2].start()

    fetches[0].start()
    fetches[1].start()
    for copy in small[3:]:
        copy.start()
    to_near = pltpu.make_async_copy(adjacency_at, adjacency, local_sem.at[0])
    to_near.start()
    for copy in small:
        copy.wait()
    place = request(x, z, k, owner, block, mine)
    project(0)
    pl.semaphore_wait(barrier, len(peers))

    started = []

    def send(src, dst, device):
        i = used[0]
        used[0] += 1
        copy = pltpu.make_async_remote_copy(
            src_ref=src,
            dst_ref=dst,
            send_sem=send_sem.at[i],
            recv_sem=recv_sem.at[i],
            device_id=device,
            device_id_type=MESH,
        )
        copy.start()
        started.append(copy)
        return copy

    def arrived(copies):
        for copy in copies:
            copy.wait_recv()

    def piece(i, count):
        return pl.ds(i * (NB // count), NB // count)

    def along_both(up_from, down_from, up_to, down_to, p):
        return [send(up_from.at[p], up_to.at[p], at_z(1)), send(down_from.at[p], down_to.at[p], at_z(-1))]

    quarters = [piece(i, 4) for i in range(4)]
    halves = [piece(i, 2) for i in range(2)]
    hop = [along_both(table_one, table_one, up_one, down_one, quarters[0])]
    asks = [send(mine, wanted_all.at[2, me], at_slab(g)) for g in range(1, GROUPS)]
    wanted_all[2, me] = mine[...]
    project(1)
    hop.append(along_both(table_one, table_one, up_one, down_one, quarters[1]))
    arrived(asks)
    asks = [send(wanted_all.at[2], wanted_all.at[2 - s], at_z(s)) for s in (1, -1, 2, -2)]
    project(2)
    project(3)
    hop.append(along_both(table_one, table_one, up_one, down_one, halves[1]))
    to_sources = pltpu.make_async_copy(table_one, sources_one.at[pl.ds(0, NB)], local_sem.at[1])
    to_sources.start()
    sort(count[0], target, source, place, listed, kept)
    to_order = pltpu.make_async_copy(listed, order, local_sem.at[13])
    to_order.start()
    to_keep = pltpu.make_async_copy(kept, keep, local_sem.at[14])
    to_keep.start()
    for i in range(4):
        project(4 + i)
    next_hop = []
    for i in range(2):
        arrived(hop[i])
    next_hop.append(along_both(up_one, down_one, up_two, down_two, halves[0]))
    arrived(asks)
    to_scalars = pltpu.make_async_copy(wanted_all, wanted, local_sem.at[2])
    to_scalars.start()
    to_scalars.wait()
    to_order.wait()
    to_keep.wait()
    arrived(hop[2])
    next_hop.append(along_both(up_one, down_one, up_two, down_two, halves[1]))

    def pick(shift, group, step, slot):
        ox, ok = member(x, k, group)
        o = row_of(x, lax.rem(z + step + NZ, NZ), k)
        return jnp.clip(wanted[2 + shift, ox * 2 + ok, 0, 2 * o + slot], 0, NB - 1)

    def pack_share(parts):
        @pl.loop(0, GROUPS)
        def _(g):
            for i, table in parts:
                for slot in range(2):
                    share[g * SHARE + 2 * i + slot] = table[pick(0, g, STEPS[i], slot)]

    def send_share(g, start, size, sources):
        at = g * SHARE + start
        return send(share.at[pl.ds(at, size)], sources.at[pl.ds(NB + at, size)], at_slab(g))

    def pack_relay(up, down):
        @pl.loop(0, GROUPS)
        def _(g):
            for side, (table, sign) in enumerate(((up, 1), (down, -1))):
                for slot in range(2):
                    relay_out[side, g * 2 + slot] = table[pick(sign, g, -2 * sign, slot)]
                relay_out[2 + side, g] = table[pick(2 * sign, g, -2 * sign, side)]

    def send_relay(layer, first):
        near, far = pl.ds(first * 2, 4), pl.ds(first, 2)
        copies = []
        for side, sign in ((0, 1), (1, -1)):
            copies.append(send(relay_out.at[2 + side, far], relay_in.at[layer, 2 + side, far], at_z(2 * sign)))
            copies.append(send(relay_out.at[side, near], relay_in.at[layer, side, near], at_z(sign)))
        return copies

    def pack_far(layer, g):
        at = g * SHARE
        share[at + 10] = relay_in[layer, 0, 2 * g]
        share[at + 11] = relay_in[layer, 0, 2 * g + 1]
        share[at + 12] = relay_in[layer, 1, 2 * g]
        share[at + 13] = relay_in[layer, 1, 2 * g + 1]
        share[at + 14] = relay_in[layer, 2, g]
        share[at + 15] = relay_in[layer, 3, g]

    def forward_far(layer, relays, sources, between):
        copies = []
        for first, then in zip(FIRSTS, between):
            arrived(relays[first])
            for g in (first, first + 1):
                pack_far(layer, g)
                if g > 0:
                    copies.append(send_share(g, 10, 6, sources))
            then()
        return copies

    def keep_own(sources, i):
        copy = pltpu.make_async_copy(
            share.at[pl.ds(0, SHARE)], sources.at[pl.ds(NB, SHARE)], local_sem.at[i]
        )
        copy.start()
        copy.wait()

    def multiply(sources):
        def some(step, total):
            for i in range(UNROLL):
                e = order[0, step * UNROLL + i]
                product = jnp.dot(
                    adjacency[jnp.clip(e & 255, 0, TILES - 1)],
                    sources[jnp.clip(e >> 8, 0, NB + GROUPS * SHARE - 1)],
                    preferred_element_type=jnp.float32,
                )
                total = total * keep[0, step * UNROLL + i] + product
                sums[step * UNROLL + i] = total
            return total

        lax.fori_loop(0, TILES // UNROLL, some, jnp.zeros((BLOCK, BLOCK), jnp.float32))

    def summed(b):
        return sums[jnp.clip(order[1, b], 0, TILES - 1)] * keep[1, b]

    def nothing():
        pass

    others = range(1, GROUPS)

    pack_share([(0, table_one), (1, up_one), (2, down_one)])
    past = []

    def start_past():
        past.append(along_both(table_past, table_past, up_past, down_past, quarters[len(past)]))

    arrived(next_hop[0])
    start_past()
    arrived(next_hop[1])
    pack_relay(up_two, down_two)
    relays = {first: send_relay(0, first) for first in FIRSTS}
    pack_share([(3, up_two), (4, down_two)])
    halo_copies = [send_share(g, 0, 10, sources_one) for g in others]

    def start_two():
        start_past()
        start_past()

    halo_copies += forward_far(
        0, relays, sources_one, (nothing, start_past, start_two, nothing)
    )
    hop = []
    for i in range(2):
        arrived(past[2 * i] + past[2 * i + 1])
        hop.append(along_both(up_past, down_past, up_past_two, down_past_two, halves[i]))
    keep_own(sources_one, 3)
    arrived(halo_copies)
    for copy in halo_copies:
        copy.wait_send()
    pack_share([(0, table_past), (1, up_past), (2, down_past)])
    last_copies = [send_share(g, 0, 6, sources_two) for g in others]
    to_near.wait()
    to_sources.wait()
    multiply(sources_one)

    @pl.loop(0, NB)
    def _(b):
        hidden[b] = jnp.maximum(summed(b) + bias_one[...], 0.0).astype(jnp.bfloat16)

    hidden_out = pltpu.make_async_copy(hidden, hidden_at, local_sem.at[15])
    hidden_out.start()
    low, high = piece(0, 2), piece(1, 2)
    from_below = [send(hidden.at[low], near_y.at[0, low], at_y(1))]
    from_above = [send(hidden.at[high], near_y.at[1, high], at_y(-1))]
    from_below.append(send(hidden.at[high], near_y.at[0, high], at_y(1)))
    from_above.append(send(hidden.at[low], near_y.at[1, low], at_y(-1)))

    for copies in relays.values():
        for copy in copies:
            copy.wait_send()
    for copies in hop:
        arrived(copies)
    pack_relay(up_past_two, down_past_two)
    relays_two = {first: send_relay(1, first) for first in FIRSTS}
    pack_share([(3, up_past_two), (4, down_past_two)])
    last_copies += [send_share(g, 6, 4, sources_two) for g in others]
    arrived([from_below[0], from_above[0]])
    across = [
        send(near_y.at[0, low], far_y.at[low], at_y(1)),
        send(near_y.at[1, high], far_y.at[high], at_y(-1)),
    ]

    def part(shift):
        return weight[pl.ds(pl.multiple_of(lax.rem(y + shift, NY) * BLOCK, BLOCK), BLOCK), :]

    def project_hidden():
        arrived([from_below[1], from_above[1], *across])

        @pl.loop(0, NB // 4)
        def _(i):
            here = pl.ds(i * 4, 4)
            total = jnp.zeros((4 * BLOCK, BLOCK), jnp.float32)
            for rows, shift in ((hidden, 0), (near_y.at[0], 3), (near_y.at[1], 1), (far_y, 2)):
                total += jnp.dot(
                    rows[here].reshape(4 * BLOCK, BLOCK),
                    part(shift),
                    preferred_element_type=jnp.float32,
                )
            sources_two[here] = total.astype(jnp.bfloat16).reshape(4, BLOCK, BLOCK)

    last_copies += forward_far(1, relays_two, sources_two, (nothing, nothing, project_hidden, nothing))
    keep_own(sources_two, 4)
    arrived(last_copies)
    multiply(sources_two)

    outs = []
    for i in range(4):

        @pl.loop(i * NB // 4, (i + 1) * NB // 4)
        def _(b):
            embedding[b] = summed(b)

        outs.append(
            pltpu.make_async_copy(embedding.at[quarters[i]], embedding_at.at[quarters[i]], local_sem.at[24 + i])
        )
        outs[i].start()
    hidden_out.wait()
    for copy in outs:
        copy.wait()
    assert used[0] == COPIES
    waited = halo_copies + [c for copies in relays.values() for c in copies]
    for copy in started:
        if not any(copy is w for w in waited):
            copy.wait_send()


def exchange(count, owner, block, target, source, bias, weight_one, weight_two, features, history, adjacency):
    def blocks(*count):
        return pltpu.VMEM((*count, BLOCK, BLOCK), jnp.bfloat16)

    return pl.pallas_call(
        exchange_kernel,
        out_shape=(
            jax.ShapeDtypeStruct((NB, BLOCK, BLOCK), jnp.bfloat16),
            jax.ShapeDtypeStruct((NB, BLOCK, BLOCK), jnp.float32),
        ),
        in_specs=[SMEM] + [ANY] * 10,
        out_specs=(ANY, ANY),
        scratch_shapes=[
            pltpu.VMEM((1, HALO), jnp.int32),
            pltpu.VMEM((1, HALO), jnp.int32),
            pltpu.VMEM((1, TILES), jnp.int32),
            pltpu.VMEM((1, TILES), jnp.int32),
            pltpu.VMEM((1, BLOCK), jnp.float32),
            pltpu.VMEM((4 * BLOCK, BLOCK), jnp.bfloat16),
            pltpu.VMEM((4 * BLOCK, BLOCK), jnp.bfloat16),
            blocks(NB),
            pltpu.VMEM((NB, BLOCK, BLOCK), jnp.float32),
            pltpu.VMEM((8, 128), jnp.int32),
            pltpu.VMEM((8, 256), jnp.int32),
            pltpu.VMEM((8, 256), jnp.float32),
            pltpu.SMEM((8, 256), jnp.int32),
            pltpu.SMEM((8, 256), jnp.float32),
            pltpu.VMEM((5, GROUPS, 8, 128), jnp.int32),
            pltpu.SMEM((5, GROUPS, 8, 128), jnp.int32),
            pltpu.VMEM((2, NB * BLOCK // 4, 4 * BLOCK), jnp.bfloat16),
            *[blocks(NB)] * 10,
            blocks(4, 2 * GROUPS),
            blocks(2, 4, 2 * GROUPS),
            blocks(GROUPS * SHARE),
            blocks(NB + GROUPS * SHARE),
            blocks(NB + GROUPS * SHARE),
            blocks(TILES),
            pltpu.VMEM((TILES, BLOCK, BLOCK), jnp.float32),
            blocks(2, NB),
            blocks(NB),
            pltpu.SemaphoreType.DMA((COPIES,)),
            pltpu.SemaphoreType.DMA((COPIES,)),
            pltpu.SemaphoreType.DMA((28,)),
        ],
        compiler_params=pltpu.CompilerParams(
            vmem_limit_bytes=60 * 2**20, collective_id=0, has_side_effects=True
        ),
        cost_estimate=pl.CostEstimate(
            flops=2 * 1024 * BLOCK**3, bytes_accessed=32 << 20, transcendentals=0
        ),
        name="exchange",
    )(
        count,
        owner,
        block,
        target,
        source,
        bias.reshape(1, BLOCK),
        weight_one,
        weight_two,
        features,
        history,
        adjacency,
    )


def local(
    features,
    history,
    weight_one,
    weight_two,
    bias_one,
    bias_two,
    adjacency,
    halo_owner,
    halo_block,
    tile_target,
    tile_source,
    tile_count,
):
    hidden, summed = exchange(
        tile_count,
        halo_owner,
        halo_block,
        tile_target,
        tile_source,
        bias_one,
        weight_one,
        weight_two,
        features,
        history,
        adjacency,
    )
    hidden = jnp.maximum(hidden.reshape(NB * BLOCK, BLOCK), 0)
    embedding = (summed.reshape(NB * BLOCK, BLOCK) + bias_two).astype(jnp.bfloat16)
    return (hidden, embedding)


def solution(mesh):
    return jax.shard_map(
        local,
        mesh=mesh,
        in_specs=(
            P("row", None),
            P("row", None),
            P(None, "col"),
            P(None, "col"),
            P("col"),
            P("col"),
            P("row", None, None),
            P("row", None),
            P("row", None),
            P("row", None),
            P("row", None),
            P("row"),
        ),
        out_specs=(P("row", "col"), P("row", "col")),
        check_vma=False,
    )
```

```python
import jax
import jax.numpy as jnp
from jax import lax
from jax.experimental import pallas as pl
from jax.experimental.pallas import tpu as pltpu
from jax.sharding import PartitionSpec as P

BLOCK = 128
NB = 32
TILES = 192
HALO = 96
NX, NZ, NY = 4, 8, 4
GROUPS = 8
SHARE = 16
PAIRS = (TILES + NB) // 2
UNROLL = 8
FIRSTS = (4, 2, 6, 0)
MESH = pl.DeviceIdType.MESH

STEPS = (0, 7, 1, 6, 2, 5, 3, 4)

SMEM = pl.BlockSpec(memory_space=pltpu.SMEM)
VMEM = pl.BlockSpec(memory_space=pltpu.VMEM)
ANY = pl.BlockSpec(memory_space=pl.ANY)


def row_of(x, z, k):
    return x * (NZ * 2) + z * 2 + k


def member(x, k, group):
    dx, dk = group // 2, group % 2
    return lax.rem(x + dx, NX), k + dk - 2 * k * dk


def lane(shape, axis):
    return lax.broadcasted_iota(jnp.int32, shape, axis)


def upright(row):
    n = row.shape[1]
    shape = (n, n)
    diagonal = lane(shape, 0) == lane(shape, 1)
    return jnp.sum(jnp.where(diagonal, row, 0), axis=1, keepdims=True)


def request(x, z, k, owner, block, mine):
    row = owner[...]
    named = upright(row)
    square = (HALO, HALO)
    earlier = lane(square, 1) < lane(square, 0)
    nth = jnp.sum(jnp.where((row == named) & earlier, 1, 0), axis=1, keepdims=True)
    code = jnp.where(named >= 0, 2 * named + nth, -1)
    slots = lane((HALO, 128), 1)
    wanted = jnp.sum(jnp.where(code == slots, upright(block[...]), 0), axis=0, keepdims=True)
    mine[...] = jnp.broadcast_to(wanted, (8, 128))
    o = jnp.maximum(named, 0)
    ox, oz, ok = o >> 4, (o >> 1) & 7, o & 1
    group = ((x - ox) & 3) * 2 + (k + ok - 2 * k * ok)
    step = (oz - z) & 7
    spot = jnp.zeros_like(o)
    for i, s in enumerate(STEPS):
        spot = jnp.where(step == s, 2 * i, spot)
    return group * SHARE + spot + jnp.minimum(nth, 1)


def sort(live, target, source, place, listed, kept):
    ids = lane((1, TILES), 1)
    s = source[...]
    slots = lane((HALO, TILES), 0)
    halo = jnp.sum(jnp.where(slots == s - NB, place, 0), axis=0, keepdims=True)
    at = jnp.where(s < NB, s, halo + NB)
    entry = upright(ids + 256 * at)
    row = jnp.where(ids < live, target[...], NB)
    goal = upright(row)
    key = row * 256 + ids
    rank = jnp.sum(jnp.where(key < upright(key), 1, 0), axis=1, keepdims=True)
    before = jnp.sum(jnp.where(row < goal, 1, 0), axis=1, keepdims=True)
    mine = goal == lane((TILES, 128), 1)
    many = jnp.sum(jnp.where(mine, 1, 0), axis=0, keepdims=True)
    pairs = (many + 1) >> 1
    square = (128, 128)
    start = jnp.sum(
        jnp.where(lane(square, 0) < lane(square, 1), upright(pairs), 0), axis=0, keepdims=True
    )
    spot = 2 * jnp.sum(jnp.where(mine, start, 0), axis=1, keepdims=True) + rank - before
    here = spot == lane((TILES, 256), 1)
    filled = jnp.sum(jnp.where(here, 1, 0), axis=0, keepdims=True)
    order = jnp.sum(jnp.where(here, entry, 0), axis=0, keepdims=True)
    listed[0:1, 0:256] = jnp.where(filled > 0, order, TILES)
    opens = (upright(start) == lane(square, 1)) & (upright(many) > 0)
    first = jnp.sum(jnp.where(opens, 1, 0), axis=0, keepdims=True)
    kept[0:1, 0:128] = jnp.where(first > 0, 0.0, 1.0)
    listed[1:2, 0:128] = jnp.maximum(start + pairs - 1, 0)
    kept[1:2, 0:128] = jnp.where(many > 0, 1.0, 0.0)


COPIES = 106


def exchange_kernel(
    count,
    owner_at,
    block_at,
    target_at,
    source_at,
    bias_at,
    first_weight_at,
    weight_at,
    features,
    history,
    adjacency_at,
    hidden_at,
    embedding_at,
    owner,
    block,
    target,
    source,
    bias_one,
    first_weight,
    weight,
    hidden,
    embedding,
    mine,
    listed,
    kept,
    order,
    keep,
    wanted_all,
    wanted,
    stage,
    table_one,
    table_past,
    up_one,
    down_one,
    up_two,
    down_two,
    up_past,
    down_past,
    up_past_two,
    down_past_two,
    relay_out,
    relay_in,
    share,
    sources_one,
    sources_two,
    adjacency,
    sums,
    near_y,
    far_y,
    send_sem,
    recv_sem,
    local_sem,
):
    row = lax.axis_index("row")
    y = lax.axis_index("col")
    x, z, k = row // 16, lax.rem(row // 2, NZ), lax.rem(row, 2)
    me = x * 2 + k
    used = [0]

    def at_z(step):
        return (row_of(x, lax.rem(z + step + NZ, NZ), k), y)

    def at_slab(group):
        ox, ok = member(x, k, group)
        return (row_of(ox, z, ok), y)

    def at_y(step):
        return (row, lax.rem(y + step + NY, NY))

    peers = [at_z(s) for s in (1, -1, 2, -2)]
    peers += [at_slab(g) for g in range(1, GROUPS)]
    peers += [at_y(s) for s in (1, -1)]

    barrier = pltpu.get_barrier_semaphore()
    for peer in peers:
        pl.semaphore_signal(barrier, inc=1, device_id=peer, device_id_type=MESH)

    small = [
        pltpu.make_async_copy(at, here, local_sem.at[16 + i])
        for i, (at, here) in enumerate(
            (
                (first_weight_at, first_weight),
                (owner_at, owner),
                (block_at, block),
                (target_at, target),
                (source_at, source),
                (bias_at, bias_one),
                (weight_at, weight),
            )
        )
    ]
    for copy in small[:3]:
        copy.start()

    rows = NB * BLOCK // 4
    pieces = [(table, w, at, i) for table, w, at in ((table_one, first_weight, features), (table_past, weight, history)) for i in range(4)]
    fetches = [
        pltpu.make_async_copy(at.at[pl.ds(i * rows, rows)], stage.at[n % 2], local_sem.at[5 + n])
        for n, (_, _, at, i) in enumerate(pieces)
    ]

    def project(n):
        table, w, _, i = pieces[n]
        fetches[n].wait()

        @pl.loop(0, NB // 8)
        def _(j):
            part = stage[n % 2, pl.ds(j * 2 * BLOCK, 2 * BLOCK)]
            product = jnp.dot(part, w[...], preferred_element_type=jnp.float32)
            table[pl.ds(i * (NB // 4) + 2 * j, 2)] = product.astype(jnp.bfloat16).reshape(2, BLOCK, BLOCK)

        if n + 2 < len(pieces):
            fetches[n + 2].start()

    fetches[0].start()
    fetches[1].start()
    for copy in small[3:]:
        copy.start()
    to_near = pltpu.make_async_copy(adjacency_at, adjacency.at[pl.ds(0, TILES)], local_sem.at[0])
    to_near.start()
    adjacency[TILES] = jnp.zeros((BLOCK, BLOCK), jnp.bfloat16)
    for copy in small:
        copy.wait()
    place = request(x, z, k, owner, block, mine)
    project(0)
    pl.semaphore_wait(barrier, len(peers))

    started = []

    def send(src, dst, device):
        i = used[0]
        used[0] += 1
        copy = pltpu.make_async_remote_copy(
            src_ref=src,
            dst_ref=dst,
            send_sem=send_sem.at[i],
            recv_sem=recv_sem.at[i],
            device_id=device,
            device_id_type=MESH,
        )
        copy.start()
        started.append(copy)
        return copy

    def arrived(copies):
        for copy in copies:
            copy.wait_recv()

    def piece(i, count):
        return pl.ds(i * (NB // count), NB // count)

    def along_both(up_from, down_from, up_to, down_to, p):
        return [send(up_from.at[p], up_to.at[p], at_z(1)), send(down_from.at[p], down_to.at[p], at_z(-1))]

    quarters = [piece(i, 4) for i in range(4)]
    halves = [piece(i, 2) for i in range(2)]
    hop = [along_both(table_one, table_one, up_one, down_one, quarters[0])]
    asks = [send(mine, wanted_all.at[2, me], at_slab(g)) for g in range(1, GROUPS)]
    wanted_all[2, me] = mine[...]
    project(1)
    hop.append(along_both(table_one, table_one, up_one, down_one, quarters[1]))
    arrived(asks)
    asks = [send(wanted_all.at[2], wanted_all.at[2 - s], at_z(s)) for s in (1, -1, 2, -2)]
    project(2)
    project(3)
    hop.append(along_both(table_one, table_one, up_one, down_one, halves[1]))
    to_sources = pltpu.make_async_copy(table_one, sources_one.at[pl.ds(0, NB)], local_sem.at[1])
    to_sources.start()
    sort(count[0], target, source, place, listed, kept)
    to_order = pltpu.make_async_copy(listed, order, local_sem.at[13])
    to_order.start()
    to_keep = pltpu.make_async_copy(kept, keep, local_sem.at[14])
    to_keep.start()
    for i in range(4):
        project(4 + i)
    next_hop = []
    for i in range(2):
        arrived(hop[i])
    next_hop.append(along_both(up_one, down_one, up_two, down_two, halves[0]))
    arrived(asks)
    to_scalars = pltpu.make_async_copy(wanted_all, wanted, local_sem.at[2])
    to_scalars.start()
    to_scalars.wait()
    to_order.wait()
    to_keep.wait()
    arrived(hop[2])
    next_hop.append(along_both(up_one, down_one, up_two, down_two, halves[1]))

    def pick(shift, group, step, slot):
        ox, ok = member(x, k, group)
        o = row_of(x, lax.rem(z + step + NZ, NZ), k)
        return jnp.clip(wanted[2 + shift, ox * 2 + ok, 0, 2 * o + slot], 0, NB - 1)

    def pack_share(parts, first=None):
        @pl.loop(0 if first is None else first, GROUPS if first is None else first + 2)
        def _(g):
            for i, table in parts:
                for slot in range(2):
                    share[g * SHARE + 2 * i + slot] = table[pick(0, g, STEPS[i], slot)]

    def send_share(g, start, size, sources):
        at = g * SHARE + start
        return send(share.at[pl.ds(at, size)], sources.at[pl.ds(NB + at, size)], at_slab(g))

    def pack_relay(up, down, first):
        @pl.loop(first, first + 2)
        def _(g):
            for side, (table, sign) in enumerate(((up, 1), (down, -1))):
                for slot in range(2):
                    relay_out[side, g * 2 + slot] = table[pick(sign, g, -2 * sign, slot)]
                relay_out[2 + side, g] = table[pick(2 * sign, g, -2 * sign, side)]

    def send_relay(layer, first):
        near, far = pl.ds(first * 2, 4), pl.ds(first, 2)
        copies = []
        for side, sign in ((0, 1), (1, -1)):
            copies.append(send(relay_out.at[2 + side, far], relay_in.at[layer, 2 + side, far], at_z(2 * sign)))
            copies.append(send(relay_out.at[side, near], relay_in.at[layer, side, near], at_z(sign)))
        return copies

    def pack_far(layer, g):
        at = g * SHARE
        share[at + 10] = relay_in[layer, 0, 2 * g]
        share[at + 11] = relay_in[layer, 0, 2 * g + 1]
        share[at + 12] = relay_in[layer, 1, 2 * g]
        share[at + 13] = relay_in[layer, 1, 2 * g + 1]
        share[at + 14] = relay_in[layer, 2, g]
        share[at + 15] = relay_in[layer, 3, g]

    def forward_far(layer, relays, sources, between):
        copies = []
        for first, then in zip(FIRSTS, between):
            arrived(relays[first])
            for g in (first, first + 1):
                pack_far(layer, g)
                if g > 0:
                    copies.append(send_share(g, 10, 6, sources))
            then()
        return copies

    def keep_own(sources, i):
        copy = pltpu.make_async_copy(
            share.at[pl.ds(0, SHARE)], sources.at[pl.ds(NB, SHARE)], local_sem.at[i]
        )
        copy.start()
        copy.wait()

    def multiply(sources):
        def tile(e):
            return adjacency[jnp.clip(e & 255, 0, TILES)]

        def origin(e):
            return sources[jnp.clip(e >> 8, 0, NB + GROUPS * SHARE - 1)]

        def some(step, total):
            for i in range(UNROLL):
                pair = step * UNROLL + i
                one, two = order[0, 2 * pair], order[0, 2 * pair + 1]
                product = jnp.dot(
                    jnp.concatenate([tile(one), tile(two)], axis=1),
                    jnp.concatenate([origin(one), origin(two)], axis=0),
                    preferred_element_type=jnp.float32,
                )
                total = total * keep[0, pair] + product
                sums[pair] = total
            return total

        lax.fori_loop(0, PAIRS // UNROLL, some, jnp.zeros((BLOCK, BLOCK), jnp.float32))

    def summed(b):
        return sums[jnp.clip(order[1, b], 0, PAIRS - 1)] * keep[1, b]

    def nothing():
        pass

    others = range(1, GROUPS)

    pack_share([(0, table_one), (1, up_one), (2, down_one)])
    past = []

    def start_past():
        past.append(along_both(table_past, table_past, up_past, down_past, quarters[len(past)]))

    arrived(next_hop[0])
    start_past()
    arrived(next_hop[1])
    relays = {}
    for first in FIRSTS:
        pack_relay(up_two, down_two, first)
        relays[first] = send_relay(0, first)
    pack_share([(3, up_two), (4, down_two)])
    halo_copies = [send_share(g, 0, 10, sources_one) for g in others]

    def start_two():
        start_past()
        start_past()

    halo_copies += forward_far(
        0, relays, sources_one, (nothing, start_past, start_two, nothing)
    )
    hop = []
    for i in range(2):
        arrived(past[2 * i] + past[2 * i + 1])
        hop.append(along_both(up_past, down_past, up_past_two, down_past_two, halves[i]))
    keep_own(sources_one, 3)
    arrived(halo_copies)
    for copy in halo_copies:
        copy.wait_send()
    pack_share([(0, table_past), (1, up_past), (2, down_past)])
    last_copies = [send_share(g, 0, 6, sources_two) for g in others]
    to_near.wait()
    to_sources.wait()
    multiply(sources_one)

    @pl.loop(0, NB)
    def _(b):
        hidden[b] = jnp.maximum(summed(b) + bias_one[...], 0.0).astype(jnp.bfloat16)

    hidden_out = pltpu.make_async_copy(hidden, hidden_at, local_sem.at[15])
    hidden_out.start()
    low, high = piece(0, 2), piece(1, 2)
    from_below = [send(hidden.at[low], near_y.at[0, low], at_y(1))]
    from_above = [send(hidden.at[high], near_y.at[1, high], at_y(-1))]
    from_below.append(send(hidden.at[high], near_y.at[0, high], at_y(1)))
    from_above.append(send(hidden.at[low], near_y.at[1, low], at_y(-1)))

    for copies in relays.values():
        for copy in copies:
            copy.wait_send()
    for copies in hop:
        arrived(copies)
    relays_two = {}
    for first in FIRSTS:
        pack_relay(up_past_two, down_past_two, first)
        relays_two[first] = send_relay(1, first)
        pack_share([(3, up_past_two), (4, down_past_two)], first)
        for g in (first, first + 1):
            if g > 0:
                last_copies.append(send_share(g, 6, 4, sources_two))
    arrived([from_below[0], from_above[0]])
    across = [
        send(near_y.at[0, low], far_y.at[low], at_y(1)),
        send(near_y.at[1, high], far_y.at[high], at_y(-1)),
    ]

    def part(shift):
        return weight[pl.ds(pl.multiple_of(lax.rem(y + shift, NY) * BLOCK, BLOCK), BLOCK), :]

    def project_hidden():
        arrived([from_below[1], from_above[1], *across])

        @pl.loop(0, NB // 4)
        def _(i):
            here = pl.ds(i * 4, 4)
            total = jnp.zeros((4 * BLOCK, BLOCK), jnp.float32)
            for rows, shift in ((hidden, 0), (near_y.at[0], 3), (near_y.at[1], 1), (far_y, 2)):
                total += jnp.dot(
                    rows[here].reshape(4 * BLOCK, BLOCK),
                    part(shift),
                    preferred_element_type=jnp.float32,
                )
            sources_two[here] = total.astype(jnp.bfloat16).reshape(4, BLOCK, BLOCK)

    last_copies += forward_far(1, relays_two, sources_two, (nothing, nothing, project_hidden, nothing))
    keep_own(sources_two, 4)
    arrived(last_copies)
    multiply(sources_two)

    outs = []
    for i in range(4):

        @pl.loop(i * NB // 4, (i + 1) * NB // 4)
        def _(b):
            embedding[b] = summed(b)

        outs.append(
            pltpu.make_async_copy(embedding.at[quarters[i]], embedding_at.at[quarters[i]], local_sem.at[24 + i])
        )
        outs[i].start()
    hidden_out.wait()
    for copy in outs:
        copy.wait()
    assert used[0] == COPIES
    waited = halo_copies + [c for copies in relays.values() for c in copies]
    for copy in started:
        if not any(copy is w for w in waited):
            copy.wait_send()


def exchange(count, owner, block, target, source, bias, weight_one, weight_two, features, history, adjacency):
    def blocks(*count):
        return pltpu.VMEM((*count, BLOCK, BLOCK), jnp.bfloat16)

    return pl.pallas_call(
        exchange_kernel,
        out_shape=(
            jax.ShapeDtypeStruct((NB, BLOCK, BLOCK), jnp.bfloat16),
            jax.ShapeDtypeStruct((NB, BLOCK, BLOCK), jnp.float32),
        ),
        in_specs=[SMEM] + [ANY] * 10,
        out_specs=(ANY, ANY),
        scratch_shapes=[
            pltpu.VMEM((1, HALO), jnp.int32),
            pltpu.VMEM((1, HALO), jnp.int32),
            pltpu.VMEM((1, TILES), jnp.int32),
            pltpu.VMEM((1, TILES), jnp.int32),
            pltpu.VMEM((1, BLOCK), jnp.float32),
            pltpu.VMEM((4 * BLOCK, BLOCK), jnp.bfloat16),
            pltpu.VMEM((4 * BLOCK, BLOCK), jnp.bfloat16),
            blocks(NB),
            pltpu.VMEM((NB, BLOCK, BLOCK), jnp.float32),
            pltpu.VMEM((8, 128), jnp.int32),
            pltpu.VMEM((8, 256), jnp.int32),
            pltpu.VMEM((8, 256), jnp.float32),
            pltpu.SMEM((8, 256), jnp.int32),
            pltpu.SMEM((8, 256), jnp.float32),
            pltpu.VMEM((5, GROUPS, 8, 128), jnp.int32),
            pltpu.SMEM((5, GROUPS, 8, 128), jnp.int32),
            pltpu.VMEM((2, NB * BLOCK // 4, 4 * BLOCK), jnp.bfloat16),
            *[blocks(NB)] * 10,
            blocks(4, 2 * GROUPS),
            blocks(2, 4, 2 * GROUPS),
            blocks(GROUPS * SHARE),
            blocks(NB + GROUPS * SHARE),
            blocks(NB + GROUPS * SHARE),
            blocks(TILES + 1),
            pltpu.VMEM((PAIRS, BLOCK, BLOCK), jnp.float32),
            blocks(2, NB),
            blocks(NB),
            pltpu.SemaphoreType.DMA((COPIES,)),
            pltpu.SemaphoreType.DMA((COPIES,)),
            pltpu.SemaphoreType.DMA((28,)),
        ],
        compiler_params=pltpu.CompilerParams(
            vmem_limit_bytes=60 * 2**20, collective_id=0, has_side_effects=True
        ),
        cost_estimate=pl.CostEstimate(
            flops=2 * 1024 * BLOCK**3, bytes_accessed=32 << 20, transcendentals=0
        ),
        name="exchange",
    )(
        count,
        owner,
        block,
        target,
        source,
        bias.reshape(1, BLOCK),
        weight_one,
        weight_two,
        features,
        history,
        adjacency,
    )


def finish_kernel(hidden_at, summed_at, bias_at, hidden, embedding, summed, value, bias, sem):
    across = pltpu.make_async_copy(hidden_at, hidden, sem.at[0])
    take = pltpu.make_async_copy(bias_at, bias, sem.at[1])
    width = NB // 4
    parts = [pl.ds(i * width, width) for i in range(4)]
    ins = [pltpu.make_async_copy(summed_at.at[p], summed.at[p], sem.at[2 + i]) for i, p in enumerate(parts)]
    outs = [pltpu.make_async_copy(value.at[p], embedding.at[p], sem.at[6 + i]) for i, p in enumerate(parts)]
    take.start()
    for copy in ins:
        copy.start()
    across.start()
    take.wait()
    for i in range(4):
        ins[i].wait()

        @pl.loop(i * width, (i + 1) * width, unroll=2)
        def _(b):
            value[b] = (summed[b] + bias[...]).astype(jnp.bfloat16)

        outs[i].start()
    for copy in outs:
        copy.wait()
    across.wait()


def finish(hidden, summed, bias):
    table = jax.ShapeDtypeStruct((NB, BLOCK, BLOCK), jnp.bfloat16)
    return pl.pallas_call(
        finish_kernel,
        out_shape=(table, table),
        in_specs=[ANY] * 3,
        out_specs=(ANY, ANY),
        scratch_shapes=[
            pltpu.VMEM((NB, BLOCK, BLOCK), jnp.float32),
            pltpu.VMEM((NB, BLOCK, BLOCK), jnp.bfloat16),
            pltpu.VMEM((1, BLOCK), jnp.float32),
            pltpu.SemaphoreType.DMA((10,)),
        ],
        compiler_params=pltpu.CompilerParams(vmem_limit_bytes=60 * 2**20),
        cost_estimate=pl.CostEstimate(flops=0, bytes_accessed=6 << 20, transcendentals=0),
        name="finish",
    )(hidden, summed, bias.reshape(1, BLOCK))


def local(
    features,
    history,
    weight_one,
    weight_two,
    bias_one,
    bias_two,
    adjacency,
    halo_owner,
    halo_block,
    tile_target,
    tile_source,
    tile_count,
):
    hidden, summed = exchange(
        tile_count,
        halo_owner,
        halo_block,
        tile_target,
        tile_source,
        bias_one,
        weight_one,
        weight_two,
        features,
        history,
        adjacency,
    )
    hidden, embedding = finish(hidden, summed, bias_two)
    return (
        hidden.reshape(NB * BLOCK, BLOCK),
        embedding.reshape(NB * BLOCK, BLOCK),
    )


def solution(mesh):
    return jax.shard_map(
        local,
        mesh=mesh,
        in_specs=(
            P("row", None),
            P("row", None),
            P(None, "col"),
            P(None, "col"),
            P("col"),
            P("col"),
            P("row", None, None),
            P("row", None),
            P("row", None),
            P("row", None),
            P("row", None),
            P("row"),
        ),
        out_specs=(P("row", "col"), P("row", "col")),
        check_vma=False,
    )
```

```python
import jax
import jax.numpy as jnp
from jax import lax
from jax.experimental import pallas as pl
from jax.experimental.pallas import tpu as pltpu
from jax.sharding import PartitionSpec as P

BLOCK = 128
NB = 32
TILES = 192
HALO = 96
NX, NZ, NY = 4, 8, 4
GROUPS = 8
SHARE = 16
PAIRS = (TILES + NB) // 2
UNROLL = 8
FIRSTS = (4, 2, 6, 0)
MESH = pl.DeviceIdType.MESH

STEPS = (0, 7, 1, 6, 2, 5, 3, 4)

SMEM = pl.BlockSpec(memory_space=pltpu.SMEM)
VMEM = pl.BlockSpec(memory_space=pltpu.VMEM)
ANY = pl.BlockSpec(memory_space=pl.ANY)


def row_of(x, z, k):
    return x * (NZ * 2) + z * 2 + k


def member(x, k, group):
    dx, dk = group // 2, group % 2
    return lax.rem(x + dx, NX), k + dk - 2 * k * dk


def lane(shape, axis):
    return lax.broadcasted_iota(jnp.int32, shape, axis)


def upright(row):
    n = row.shape[1]
    shape = (n, n)
    diagonal = lane(shape, 0) == lane(shape, 1)
    return jnp.sum(jnp.where(diagonal, row, 0), axis=1, keepdims=True)


def request(x, z, k, owner, block, mine):
    row = owner[...]
    named = upright(row)
    square = (HALO, HALO)
    earlier = lane(square, 1) < lane(square, 0)
    nth = jnp.sum(jnp.where((row == named) & earlier, 1, 0), axis=1, keepdims=True)
    code = jnp.where(named >= 0, 2 * named + nth, -1)
    slots = lane((HALO, 128), 1)
    wanted = jnp.sum(jnp.where(code == slots, upright(block[...]), 0), axis=0, keepdims=True)
    mine[...] = jnp.broadcast_to(wanted, (8, 128))
    o = jnp.maximum(named, 0)
    ox, oz, ok = o >> 4, (o >> 1) & 7, o & 1
    group = ((x - ox) & 3) * 2 + (k + ok - 2 * k * ok)
    step = (oz - z) & 7
    spot = jnp.zeros_like(o)
    for i, s in enumerate(STEPS):
        spot = jnp.where(step == s, 2 * i, spot)
    return group * SHARE + spot + jnp.minimum(nth, 1)


def sort(live, target, source, place, listed, kept):
    ids = lane((1, TILES), 1)
    s = source[...]
    slots = lane((HALO, TILES), 0)
    halo = jnp.sum(jnp.where(slots == s - NB, place, 0), axis=0, keepdims=True)
    at = jnp.where(s < NB, s, halo + NB)
    entry = upright(ids + 256 * at)
    row = jnp.where(ids < live, target[...], NB)
    goal = upright(row)
    key = row * 256 + ids
    rank = jnp.sum(jnp.where(key < upright(key), 1, 0), axis=1, keepdims=True)
    before = jnp.sum(jnp.where(row < goal, 1, 0), axis=1, keepdims=True)
    mine = goal == lane((TILES, 128), 1)
    many = jnp.sum(jnp.where(mine, 1, 0), axis=0, keepdims=True)
    pairs = (many + 1) >> 1
    square = (128, 128)
    start = jnp.sum(
        jnp.where(lane(square, 0) < lane(square, 1), upright(pairs), 0), axis=0, keepdims=True
    )
    spot = 2 * jnp.sum(jnp.where(mine, start, 0), axis=1, keepdims=True) + rank - before
    here = spot == lane((TILES, 256), 1)
    filled = jnp.sum(jnp.where(here, 1, 0), axis=0, keepdims=True)
    order = jnp.sum(jnp.where(here, entry, 0), axis=0, keepdims=True)
    listed[0:1, 0:256] = jnp.where(filled > 0, order, TILES)
    opens = (upright(start) == lane(square, 1)) & (upright(many) > 0)
    first = jnp.sum(jnp.where(opens, 1, 0), axis=0, keepdims=True)
    kept[0:1, 0:128] = jnp.where(first > 0, 0.0, 1.0)
    listed[1:2, 0:128] = jnp.maximum(start + pairs - 1, 0)
    kept[1:2, 0:128] = jnp.where(many > 0, 1.0, 0.0)


COPIES = 106


def exchange_kernel(
    count,
    owner_at,
    block_at,
    target_at,
    source_at,
    bias_one_at,
    bias_two_at,
    first_weight_at,
    weight_at,
    features,
    history,
    adjacency_at,
    hidden_at,
    embedding_at,
    owner,
    block,
    target,
    source,
    bias_one,
    bias_two,
    first_weight,
    weight,
    hidden,
    embedding,
    mine,
    listed,
    kept,
    order,
    keep,
    wanted_all,
    wanted,
    stage,
    table_one,
    table_past,
    up_one,
    down_one,
    up_two,
    down_two,
    up_past,
    down_past,
    up_past_two,
    down_past_two,
    relay_out,
    relay_in,
    share,
    sources_one,
    sources_two,
    adjacency,
    sums,
    near_y,
    far_y,
    send_sem,
    recv_sem,
    local_sem,
):
    row = lax.axis_index("row")
    y = lax.axis_index("col")
    x, z, k = row // 16, lax.rem(row // 2, NZ), lax.rem(row, 2)
    me = x * 2 + k
    used = [0]

    def at_z(step):
        return (row_of(x, lax.rem(z + step + NZ, NZ), k), y)

    def at_slab(group):
        ox, ok = member(x, k, group)
        return (row_of(ox, z, ok), y)

    def at_y(step):
        return (row, lax.rem(y + step + NY, NY))

    peers = [at_z(s) for s in (1, -1, 2, -2)]
    peers += [at_slab(g) for g in range(1, GROUPS)]
    peers += [at_y(s) for s in (1, -1)]

    barrier = pltpu.get_barrier_semaphore()
    for peer in peers:
        pl.semaphore_signal(barrier, inc=1, device_id=peer, device_id_type=MESH)

    small = [
        pltpu.make_async_copy(at, here, local_sem.at[16 + i])
        for i, (at, here) in enumerate(
            (
                (first_weight_at, first_weight),
                (owner_at, owner),
                (block_at, block),
                (target_at, target),
                (source_at, source),
                (bias_one_at, bias_one),
                (bias_two_at, bias_two),
                (weight_at, weight),
            )
        )
    ]
    for copy in small[:3]:
        copy.start()

    rows = NB * BLOCK // 4
    pieces = [(table, w, at, i) for table, w, at in ((table_one, first_weight, features), (table_past, weight, history)) for i in range(4)]
    fetches = [
        pltpu.make_async_copy(at.at[pl.ds(i * rows, rows)], stage.at[n % 2], local_sem.at[5 + n])
        for n, (_, _, at, i) in enumerate(pieces)
    ]

    def project(n):
        table, w, _, i = pieces[n]
        fetches[n].wait()

        @pl.loop(0, NB // 8)
        def _(j):
            part = stage[n % 2, pl.ds(j * 2 * BLOCK, 2 * BLOCK)]
            product = jnp.dot(part, w[...], preferred_element_type=jnp.float32)
            table[pl.ds(i * (NB // 4) + 2 * j, 2)] = product.astype(jnp.bfloat16).reshape(2, BLOCK, BLOCK)

        if n + 2 < len(pieces):
            fetches[n + 2].start()

    fetches[0].start()
    fetches[1].start()
    for copy in small[3:]:
        copy.start()
    to_near = pltpu.make_async_copy(adjacency_at, adjacency.at[pl.ds(0, TILES)], local_sem.at[0])
    to_near.start()
    adjacency[TILES] = jnp.zeros((BLOCK, BLOCK), jnp.bfloat16)
    for copy in small:
        copy.wait()
    place = request(x, z, k, owner, block, mine)
    project(0)
    pl.semaphore_wait(barrier, len(peers))

    started = []

    def send(src, dst, device):
        i = used[0]
        used[0] += 1
        copy = pltpu.make_async_remote_copy(
            src_ref=src,
            dst_ref=dst,
            send_sem=send_sem.at[i],
            recv_sem=recv_sem.at[i],
            device_id=device,
            device_id_type=MESH,
        )
        copy.start()
        started.append(copy)
        return copy

    def arrived(copies):
        for copy in copies:
            copy.wait_recv()

    def piece(i, count):
        return pl.ds(i * (NB // count), NB // count)

    def along_both(up_from, down_from, up_to, down_to, p):
        return [send(up_from.at[p], up_to.at[p], at_z(1)), send(down_from.at[p], down_to.at[p], at_z(-1))]

    quarters = [piece(i, 4) for i in range(4)]
    halves = [piece(i, 2) for i in range(2)]
    hop = [along_both(table_one, table_one, up_one, down_one, quarters[0])]
    asks = [send(mine, wanted_all.at[2, me], at_slab(g)) for g in range(1, GROUPS)]
    wanted_all[2, me] = mine[...]
    project(1)
    hop.append(along_both(table_one, table_one, up_one, down_one, quarters[1]))
    arrived(asks)
    asks = [send(wanted_all.at[2], wanted_all.at[2 - s], at_z(s)) for s in (1, -1, 2, -2)]
    project(2)
    project(3)
    hop.append(along_both(table_one, table_one, up_one, down_one, halves[1]))
    to_sources = pltpu.make_async_copy(table_one, sources_one.at[pl.ds(0, NB)], local_sem.at[1])
    to_sources.start()
    sort(count[0], target, source, place, listed, kept)
    to_order = pltpu.make_async_copy(listed, order, local_sem.at[13])
    to_order.start()
    to_keep = pltpu.make_async_copy(kept, keep, local_sem.at[14])
    to_keep.start()
    for i in range(4):
        project(4 + i)
    next_hop = []
    for i in range(2):
        arrived(hop[i])
    next_hop.append(along_both(up_one, down_one, up_two, down_two, halves[0]))
    arrived(asks)
    to_scalars = pltpu.make_async_copy(wanted_all, wanted, local_sem.at[2])
    to_scalars.start()
    to_scalars.wait()
    to_order.wait()
    to_keep.wait()
    arrived(hop[2])
    next_hop.append(along_both(up_one, down_one, up_two, down_two, halves[1]))

    def pick(shift, group, step, slot):
        ox, ok = member(x, k, group)
        o = row_of(x, lax.rem(z + step + NZ, NZ), k)
        return jnp.clip(wanted[2 + shift, ox * 2 + ok, 0, 2 * o + slot], 0, NB - 1)

    def pack_share(parts, first=None):
        @pl.loop(0 if first is None else first, GROUPS if first is None else first + 2)
        def _(g):
            for i, table in parts:
                for slot in range(2):
                    share[g * SHARE + 2 * i + slot] = table[pick(0, g, STEPS[i], slot)]

    def send_share(g, start, size, sources):
        at = g * SHARE + start
        return send(share.at[pl.ds(at, size)], sources.at[pl.ds(NB + at, size)], at_slab(g))

    def pack_relay(up, down, first):
        @pl.loop(first, first + 2)
        def _(g):
            for side, (table, sign) in enumerate(((up, 1), (down, -1))):
                for slot in range(2):
                    relay_out[side, g * 2 + slot] = table[pick(sign, g, -2 * sign, slot)]
                relay_out[2 + side, g] = table[pick(2 * sign, g, -2 * sign, side)]

    def send_relay(layer, first):
        near, far = pl.ds(first * 2, 4), pl.ds(first, 2)
        copies = []
        for side, sign in ((0, 1), (1, -1)):
            copies.append(send(relay_out.at[2 + side, far], relay_in.at[layer, 2 + side, far], at_z(2 * sign)))
            copies.append(send(relay_out.at[side, near], relay_in.at[layer, side, near], at_z(sign)))
        return copies

    def pack_far(layer, g):
        at = g * SHARE
        share[at + 10] = relay_in[layer, 0, 2 * g]
        share[at + 11] = relay_in[layer, 0, 2 * g + 1]
        share[at + 12] = relay_in[layer, 1, 2 * g]
        share[at + 13] = relay_in[layer, 1, 2 * g + 1]
        share[at + 14] = relay_in[layer, 2, g]
        share[at + 15] = relay_in[layer, 3, g]

    def forward_far(layer, relays, sources, between):
        copies = []
        for first, then in zip(FIRSTS, between):
            arrived(relays[first])
            for g in (first, first + 1):
                pack_far(layer, g)
                if g > 0:
                    copies.append(send_share(g, 10, 6, sources))
            then()
        return copies

    def keep_own(sources, i):
        copy = pltpu.make_async_copy(
            share.at[pl.ds(0, SHARE)], sources.at[pl.ds(NB, SHARE)], local_sem.at[i]
        )
        copy.start()
        copy.wait()

    def multiply(sources):
        def tile(e):
            return adjacency[jnp.clip(e & 255, 0, TILES)]

        def origin(e):
            return sources[jnp.clip(e >> 8, 0, NB + GROUPS * SHARE - 1)]

        def some(step, total):
            for i in range(UNROLL):
                pair = step * UNROLL + i
                one, two = order[0, 2 * pair], order[0, 2 * pair + 1]
                product = jnp.dot(
                    jnp.concatenate([tile(one), tile(two)], axis=1),
                    jnp.concatenate([origin(one), origin(two)], axis=0),
                    preferred_element_type=jnp.float32,
                )
                total = total * keep[0, pair] + product
                sums[pair] = total
            return total

        lax.fori_loop(0, PAIRS // UNROLL, some, jnp.zeros((BLOCK, BLOCK), jnp.float32))

    def summed(b):
        return sums[jnp.clip(order[1, b], 0, PAIRS - 1)] * keep[1, b]

    def nothing():
        pass

    others = range(1, GROUPS)

    pack_share([(0, table_one), (1, up_one), (2, down_one)])
    past = []

    def start_past():
        past.append(along_both(table_past, table_past, up_past, down_past, quarters[len(past)]))

    arrived(next_hop[0])
    start_past()
    arrived(next_hop[1])
    relays = {}
    for first in FIRSTS:
        pack_relay(up_two, down_two, first)
        relays[first] = send_relay(0, first)
    pack_share([(3, up_two), (4, down_two)])
    halo_copies = [send_share(g, 0, 10, sources_one) for g in others]

    def start_two():
        start_past()
        start_past()

    halo_copies += forward_far(
        0, relays, sources_one, (nothing, start_past, start_two, nothing)
    )
    hop = []
    for i in range(2):
        arrived(past[2 * i] + past[2 * i + 1])
        hop.append(along_both(up_past, down_past, up_past_two, down_past_two, halves[i]))
    keep_own(sources_one, 3)
    arrived(halo_copies)
    for copy in halo_copies:
        copy.wait_send()
    pack_share([(0, table_past), (1, up_past), (2, down_past)])
    last_copies = [send_share(g, 0, 6, sources_two) for g in others]
    to_near.wait()
    to_sources.wait()
    multiply(sources_one)

    @pl.loop(0, NB)
    def _(b):
        hidden[b] = jnp.maximum(summed(b) + bias_one[...], 0.0).astype(jnp.bfloat16)

    hidden_out = pltpu.make_async_copy(hidden, hidden_at, local_sem.at[15])
    hidden_out.start()
    low, high = piece(0, 2), piece(1, 2)
    from_below = [send(hidden.at[low], near_y.at[0, low], at_y(1))]
    from_above = [send(hidden.at[high], near_y.at[1, high], at_y(-1))]
    from_below.append(send(hidden.at[high], near_y.at[0, high], at_y(1)))
    from_above.append(send(hidden.at[low], near_y.at[1, low], at_y(-1)))

    for copies in relays.values():
        for copy in copies:
            copy.wait_send()
    for copies in hop:
        arrived(copies)
    relays_two = {}
    for first in FIRSTS:
        pack_relay(up_past_two, down_past_two, first)
        relays_two[first] = send_relay(1, first)
        pack_share([(3, up_past_two), (4, down_past_two)], first)
        for g in (first, first + 1):
            if g > 0:
                last_copies.append(send_share(g, 6, 4, sources_two))
    arrived([from_below[0], from_above[0]])
    across = [
        send(near_y.at[0, low], far_y.at[low], at_y(1)),
        send(near_y.at[1, high], far_y.at[high], at_y(-1)),
    ]

    def part(shift):
        return weight[pl.ds(pl.multiple_of(lax.rem(y + shift, NY) * BLOCK, BLOCK), BLOCK), :]

    def project_hidden():
        arrived([from_below[1], from_above[1], *across])

        @pl.loop(0, NB // 4)
        def _(i):
            here = pl.ds(i * 4, 4)
            total = jnp.zeros((4 * BLOCK, BLOCK), jnp.float32)
            for rows, shift in ((hidden, 0), (near_y.at[0], 3), (near_y.at[1], 1), (far_y, 2)):
                total += jnp.dot(
                    rows[here].reshape(4 * BLOCK, BLOCK),
                    part(shift),
                    preferred_element_type=jnp.float32,
                )
            sources_two[here] = total.astype(jnp.bfloat16).reshape(4, BLOCK, BLOCK)

    last_copies += forward_far(1, relays_two, sources_two, (nothing, nothing, project_hidden, nothing))
    keep_own(sources_two, 4)
    arrived(last_copies)
    multiply(sources_two)

    outs = []
    for i in range(4):

        @pl.loop(i * NB // 4, (i + 1) * NB // 4)
        def _(b):
            embedding[b] = (summed(b) + bias_two[...]).astype(jnp.bfloat16)

        outs.append(
            pltpu.make_async_copy(embedding.at[quarters[i]], embedding_at.at[quarters[i]], local_sem.at[24 + i])
        )
        outs[i].start()
    hidden_out.wait()
    for copy in outs:
        copy.wait()
    assert used[0] == COPIES
    waited = halo_copies + [c for copies in relays.values() for c in copies]
    for copy in started:
        if not any(copy is w for w in waited):
            copy.wait_send()


def exchange(count, owner, block, target, source, bias_one, bias_two, weight_one, weight_two, features, history, adjacency):
    def blocks(*count):
        return pltpu.VMEM((*count, BLOCK, BLOCK), jnp.bfloat16)

    return pl.pallas_call(
        exchange_kernel,
        out_shape=(jax.ShapeDtypeStruct((NB, BLOCK, BLOCK), jnp.bfloat16),) * 2,
        in_specs=[SMEM] + [ANY] * 11,
        out_specs=(ANY, ANY),
        scratch_shapes=[
            pltpu.VMEM((1, HALO), jnp.int32),
            pltpu.VMEM((1, HALO), jnp.int32),
            pltpu.VMEM((1, TILES), jnp.int32),
            pltpu.VMEM((1, TILES), jnp.int32),
            pltpu.VMEM((1, BLOCK), jnp.float32),
            pltpu.VMEM((1, BLOCK), jnp.float32),
            pltpu.VMEM((4 * BLOCK, BLOCK), jnp.bfloat16),
            pltpu.VMEM((4 * BLOCK, BLOCK), jnp.bfloat16),
            blocks(NB),
            blocks(NB),
            pltpu.VMEM((8, 128), jnp.int32),
            pltpu.VMEM((8, 256), jnp.int32),
            pltpu.VMEM((8, 256), jnp.float32),
            pltpu.SMEM((8, 256), jnp.int32),
            pltpu.SMEM((8, 256), jnp.float32),
            pltpu.VMEM((5, GROUPS, 8, 128), jnp.int32),
            pltpu.SMEM((5, GROUPS, 8, 128), jnp.int32),
            pltpu.VMEM((2, NB * BLOCK // 4, 4 * BLOCK), jnp.bfloat16),
            *[blocks(NB)] * 10,
            blocks(4, 2 * GROUPS),
            blocks(2, 4, 2 * GROUPS),
            blocks(GROUPS * SHARE),
            blocks(NB + GROUPS * SHARE),
            blocks(NB + GROUPS * SHARE),
            blocks(TILES + 1),
            pltpu.VMEM((PAIRS, BLOCK, BLOCK), jnp.float32),
            blocks(2, NB),
            blocks(NB),
            pltpu.SemaphoreType.DMA((COPIES,)),
            pltpu.SemaphoreType.DMA((COPIES,)),
            pltpu.SemaphoreType.DMA((28,)),
        ],
        compiler_params=pltpu.CompilerParams(
            vmem_limit_bytes=60 * 2**20, collective_id=0, has_side_effects=True
        ),
        cost_estimate=pl.CostEstimate(
            flops=2 * 1024 * BLOCK**3, bytes_accessed=32 << 20, transcendentals=0
        ),
        name="exchange",
    )(
        count,
        owner,
        block,
        target,
        source,
        bias_one.reshape(1, BLOCK),
        bias_two.reshape(1, BLOCK),
        weight_one,
        weight_two,
        features,
        history,
        adjacency,
    )


def finish_kernel(hidden_at, embedding_at, hidden, embedding, held, sem):
    ins, outs = [], []
    for i, (at, to) in enumerate(((hidden_at, hidden), (embedding_at, embedding))):
        for j in range(2):
            part = pl.ds(j * (NB // 2), NB // 2)
            n = 2 * i + j
            ins.append(pltpu.make_async_copy(at.at[part], held.at[n], sem.at[n]))
            outs.append(pltpu.make_async_copy(held.at[n], to.at[part], sem.at[4 + n]))
    for copy in ins:
        copy.start()
    for come, go in zip(ins, outs):
        come.wait()
        go.start()
    for copy in outs:
        copy.wait()


def finish(hidden, embedding):
    table = jax.ShapeDtypeStruct((NB, BLOCK, BLOCK), jnp.bfloat16)
    return pl.pallas_call(
        finish_kernel,
        out_shape=(table, table),
        in_specs=[ANY] * 2,
        out_specs=(ANY, ANY),
        scratch_shapes=[
            pltpu.VMEM((4, NB // 2, BLOCK, BLOCK), jnp.bfloat16),
            pltpu.SemaphoreType.DMA((8,)),
        ],
        compiler_params=pltpu.CompilerParams(vmem_limit_bytes=60 * 2**20),
        cost_estimate=pl.CostEstimate(flops=0, bytes_accessed=4 << 20, transcendentals=0),
        name="finish",
    )(hidden, embedding)


def local(
    features,
    history,
    weight_one,
    weight_two,
    bias_one,
    bias_two,
    adjacency,
    halo_owner,
    halo_block,
    tile_target,
    tile_source,
    tile_count,
):
    hidden, embedding = exchange(
        tile_count,
        halo_owner,
        halo_block,
        tile_target,
        tile_source,
        bias_one,
        bias_two,
        weight_one,
        weight_two,
        features,
        history,
        adjacency,
    )
    hidden, embedding = finish(hidden, embedding)
    return (
        hidden.reshape(NB * BLOCK, BLOCK),
        embedding.reshape(NB * BLOCK, BLOCK),
    )


def solution(mesh):
    return jax.shard_map(
        local,
        mesh=mesh,
        in_specs=(
            P("row", None),
            P("row", None),
            P(None, "col"),
            P(None, "col"),
            P("col"),
            P("col"),
            P("row", None, None),
            P("row", None),
            P("row", None),
            P("row", None),
            P("row", None),
            P("row"),
        ),
        out_specs=(P("row", "col"), P("row", "col")),
        check_vma=False,
    )
```

```python
import jax
import jax.numpy as jnp
from jax import lax
from jax.experimental import pallas as pl
from jax.experimental.pallas import tpu as pltpu
from jax.sharding import PartitionSpec as P

BLOCK = 128
NB = 32
TILES = 192
HALO = 96
NX, NZ, NY = 4, 8, 4
GROUPS = 8
SHARE = 16
PAIRS = (TILES + NB) // 2
UNROLL = 8
EARLY = (4, 5)
FIRSTS = (4, 2, 6, 0)
MESH = pl.DeviceIdType.MESH

STEPS = (0, 7, 1, 6, 2, 5, 3, 4)

SMEM = pl.BlockSpec(memory_space=pltpu.SMEM)
VMEM = pl.BlockSpec(memory_space=pltpu.VMEM)
ANY = pl.BlockSpec(memory_space=pl.ANY)


def row_of(x, z, k):
    return x * (NZ * 2) + z * 2 + k


def member(x, k, group):
    dx, dk = group // 2, group % 2
    return lax.rem(x + dx, NX), k + dk - 2 * k * dk


def lane(shape, axis):
    return lax.broadcasted_iota(jnp.int32, shape, axis)


def upright(row):
    n = row.shape[1]
    shape = (n, n)
    diagonal = lane(shape, 0) == lane(shape, 1)
    return jnp.sum(jnp.where(diagonal, row, 0), axis=1, keepdims=True)


def request(x, z, k, owner, block, mine):
    row = owner[...]
    named = upright(row)
    square = (HALO, HALO)
    earlier = lane(square, 1) < lane(square, 0)
    nth = jnp.sum(jnp.where((row == named) & earlier, 1, 0), axis=1, keepdims=True)
    code = jnp.where(named >= 0, 2 * named + nth, -1)
    slots = lane((HALO, 128), 1)
    wanted = jnp.sum(jnp.where(code == slots, upright(block[...]), 0), axis=0, keepdims=True)
    mine[...] = jnp.broadcast_to(wanted, (8, 128))
    o = jnp.maximum(named, 0)
    ox, oz, ok = o >> 4, (o >> 1) & 7, o & 1
    group = ((x - ox) & 3) * 2 + (k + ok - 2 * k * ok)
    step = (oz - z) & 7
    spot = jnp.zeros_like(o)
    for i, s in enumerate(STEPS):
        spot = jnp.where(step == s, 2 * i, spot)
    return group * SHARE + spot + jnp.minimum(nth, 1)


def sort(live, target, source, place, listed, kept):
    ids = lane((1, TILES), 1)
    s = source[...]
    slots = lane((HALO, TILES), 0)
    halo = jnp.sum(jnp.where(slots == s - NB, place, 0), axis=0, keepdims=True)
    at = jnp.where(s < NB, s, halo + NB)
    entry = upright(ids + 256 * at)
    row = jnp.where(ids < live, target[...], NB)
    goal = upright(row)
    key = row * 256 + ids
    rank = jnp.sum(jnp.where(key < upright(key), 1, 0), axis=1, keepdims=True)
    before = jnp.sum(jnp.where(row < goal, 1, 0), axis=1, keepdims=True)
    mine = goal == lane((TILES, 128), 1)
    many = jnp.sum(jnp.where(mine, 1, 0), axis=0, keepdims=True)
    pairs = (many + 1) >> 1
    square = (128, 128)
    start = jnp.sum(
        jnp.where(lane(square, 0) < lane(square, 1), upright(pairs), 0), axis=0, keepdims=True
    )
    spot = 2 * jnp.sum(jnp.where(mine, start, 0), axis=1, keepdims=True) + rank - before
    here = spot == lane((TILES, 256), 1)
    filled = jnp.sum(jnp.where(here, 1, 0), axis=0, keepdims=True)
    order = jnp.sum(jnp.where(here, entry, 0), axis=0, keepdims=True)
    listed[0:1, 0:256] = jnp.where(filled > 0, order, TILES)
    opens = (upright(start) == lane(square, 1)) & (upright(many) > 0)
    first = jnp.sum(jnp.where(opens, 1, 0), axis=0, keepdims=True)
    kept[0:1, 0:128] = jnp.where(first > 0, 0.0, 1.0)
    listed[1:2, 0:128] = jnp.maximum(start + pairs - 1, 0)
    kept[1:2, 0:128] = jnp.where(many > 0, 1.0, 0.0)


COPIES = 108


def exchange_kernel(
    count,
    owner_at,
    block_at,
    target_at,
    source_at,
    bias_one_at,
    bias_two_at,
    first_weight_at,
    weight_at,
    features,
    history,
    adjacency_at,
    hidden_at,
    embedding_at,
    owner,
    block,
    target,
    source,
    bias_one,
    bias_two,
    first_weight,
    weight,
    hidden,
    embedding,
    mine,
    listed,
    kept,
    order,
    keep,
    wanted_all,
    wanted,
    stage,
    table_one,
    table_past,
    up_one,
    down_one,
    up_two,
    down_two,
    up_past,
    down_past,
    up_past_two,
    down_past_two,
    early_out,
    early_in,
    relay_out,
    relay_in,
    share,
    sources_one,
    sources_two,
    adjacency,
    sums,
    near_y,
    far_y,
    send_sem,
    recv_sem,
    local_sem,
):
    row = lax.axis_index("row")
    y = lax.axis_index("col")
    x, z, k = row // 16, lax.rem(row // 2, NZ), lax.rem(row, 2)
    me = x * 2 + k
    used = [0]

    def at_z(step):
        return (row_of(x, lax.rem(z + step + NZ, NZ), k), y)

    def at_slab(group):
        ox, ok = member(x, k, group)
        return (row_of(ox, z, ok), y)

    def at_y(step):
        return (row, lax.rem(y + step + NY, NY))

    peers = [at_z(s) for s in (1, -1, 2, -2)]
    peers += [at_slab(g) for g in range(1, GROUPS)]
    peers += [at_y(s) for s in (1, -1)]

    barrier = pltpu.get_barrier_semaphore()
    for peer in peers:
        pl.semaphore_signal(barrier, inc=1, device_id=peer, device_id_type=MESH)

    small = [
        pltpu.make_async_copy(at, here, local_sem.at[16 + i])
        for i, (at, here) in enumerate(
            (
                (first_weight_at, first_weight),
                (owner_at, owner),
                (block_at, block),
                (target_at, target),
                (source_at, source),
                (bias_one_at, bias_one),
                (bias_two_at, bias_two),
                (weight_at, weight),
            )
        )
    ]
    for copy in small[:3]:
        copy.start()

    rows = NB * BLOCK // 4
    pieces = [(table, w, at, i) for table, w, at in ((table_one, first_weight, features), (table_past, weight, history)) for i in range(4)]
    fetches = [
        pltpu.make_async_copy(at.at[pl.ds(i * rows, rows)], stage.at[n % 2], local_sem.at[5 + n])
        for n, (_, _, at, i) in enumerate(pieces)
    ]

    def project(n):
        table, w, _, i = pieces[n]
        fetches[n].wait()

        @pl.loop(0, NB // 8)
        def _(j):
            part = stage[n % 2, pl.ds(j * 2 * BLOCK, 2 * BLOCK)]
            product = jnp.dot(part, w[...], preferred_element_type=jnp.float32)
            table[pl.ds(i * (NB // 4) + 2 * j, 2)] = product.astype(jnp.bfloat16).reshape(2, BLOCK, BLOCK)

        if n + 2 < len(pieces):
            fetches[n + 2].start()

    fetches[0].start()
    fetches[1].start()
    for copy in small[3:]:
        copy.start()
    to_near = pltpu.make_async_copy(adjacency_at, adjacency.at[pl.ds(0, TILES)], local_sem.at[0])
    to_near.start()
    adjacency[TILES] = jnp.zeros((BLOCK, BLOCK), jnp.bfloat16)
    for copy in small:
        copy.wait()
    place = request(x, z, k, owner, block, mine)
    project(0)
    pl.semaphore_wait(barrier, len(peers))

    started = []

    def send(src, dst, device):
        i = used[0]
        used[0] += 1
        copy = pltpu.make_async_remote_copy(
            src_ref=src,
            dst_ref=dst,
            send_sem=send_sem.at[i],
            recv_sem=recv_sem.at[i],
            device_id=device,
            device_id_type=MESH,
        )
        copy.start()
        started.append(copy)
        return copy

    def arrived(copies):
        for copy in copies:
            copy.wait_recv()

    def piece(i, count):
        return pl.ds(i * (NB // count), NB // count)

    def along_both(up_from, down_from, up_to, down_to, p):
        return [send(up_from.at[p], up_to.at[p], at_z(1)), send(down_from.at[p], down_to.at[p], at_z(-1))]

    quarters = [piece(i, 4) for i in range(4)]
    halves = [piece(i, 2) for i in range(2)]
    hop = [along_both(table_one, table_one, up_one, down_one, quarters[0])]
    asks = [send(mine, wanted_all.at[2, me], at_slab(g)) for g in range(1, GROUPS)]
    wanted_all[2, me] = mine[...]
    project(1)
    hop.append(along_both(table_one, table_one, up_one, down_one, quarters[1]))
    arrived(asks)
    asks = [send(wanted_all.at[2], wanted_all.at[2 - s], at_z(s)) for s in (1, -1, 2, -2)]
    project(2)
    project(3)
    hop.append(along_both(table_one, table_one, up_one, down_one, halves[1]))
    to_sources = pltpu.make_async_copy(table_one, sources_one.at[pl.ds(0, NB)], local_sem.at[1])
    to_sources.start()
    sort(count[0], target, source, place, listed, kept)
    to_order = pltpu.make_async_copy(listed, order, local_sem.at[13])
    to_order.start()
    to_keep = pltpu.make_async_copy(kept, keep, local_sem.at[14])
    to_keep.start()
    for i in range(4):
        project(4 + i)
    next_hop = []
    for i in range(2):
        arrived(hop[i])
    next_hop.append(along_both(up_one, down_one, up_two, down_two, halves[0]))
    arrived(asks)
    to_scalars = pltpu.make_async_copy(wanted_all, wanted, local_sem.at[2])
    to_scalars.start()
    to_scalars.wait()
    to_order.wait()
    to_keep.wait()
    arrived(hop[2])
    next_hop.append(along_both(up_one, down_one, up_two, down_two, halves[1]))

    def pick(shift, group, step, slot):
        ox, ok = member(x, k, group)
        o = row_of(x, lax.rem(z + step + NZ, NZ), k)
        return jnp.clip(wanted[2 + shift, ox * 2 + ok, 0, 2 * o + slot], 0, NB - 1)

    def pack_share(parts, first=None):
        @pl.loop(0 if first is None else first, GROUPS if first is None else first + 2)
        def _(g):
            for i, table in parts:
                for slot in range(2):
                    share[g * SHARE + 2 * i + slot] = table[pick(0, g, STEPS[i], slot)]

    def send_share(g, start, size, sources):
        at = g * SHARE + start
        return send(share.at[pl.ds(at, size)], sources.at[pl.ds(NB + at, size)], at_slab(g))

    def pack_relay(up, down, first):
        @pl.loop(first, first + 2)
        def _(g):
            for side, (table, sign) in enumerate(((up, 1), (down, -1))):
                for slot in range(2):
                    relay_out[side, g * 2 + slot] = table[pick(sign, g, -2 * sign, slot)]
                relay_out[2 + side, g] = table[pick(2 * sign, g, -2 * sign, side)]

    def send_relay(layer, first):
        near, far = pl.ds(first * 2, 4), pl.ds(first, 2)
        copies = []
        for side, sign in ((0, 1), (1, -1)):
            copies.append(send(relay_out.at[2 + side, far], relay_in.at[layer, 2 + side, far], at_z(2 * sign)))
            copies.append(send(relay_out.at[side, near], relay_in.at[layer, side, near], at_z(sign)))
        return copies

    def pack_far(layer, g):
        at = g * SHARE
        share[at + 10] = relay_in[layer, 0, 2 * g]
        share[at + 11] = relay_in[layer, 0, 2 * g + 1]
        share[at + 12] = relay_in[layer, 1, 2 * g]
        share[at + 13] = relay_in[layer, 1, 2 * g + 1]
        share[at + 14] = relay_in[layer, 2, g]
        share[at + 15] = relay_in[layer, 3, g]

    def send_early():
        for side, (table, sign) in enumerate(((up_past, 1), (down_past, -1))):
            for g in EARLY:
                for slot in range(2):
                    early_out[side, (g - EARLY[0]) * 2 + slot] = table[pick(sign, g, -sign, slot)]
        return [
            send(early_out.at[0], early_in.at[0], at_z(1)),
            send(early_out.at[1], early_in.at[1], at_z(-1)),
        ]

    def forward_early(copies):
        arrived(copies)
        for g in EARLY:
            for slot in range(2):
                share[g * SHARE + 6 + slot] = early_in[0, (g - EARLY[0]) * 2 + slot]
                share[g * SHARE + 8 + slot] = early_in[1, (g - EARLY[0]) * 2 + slot]
        return [send_share(g, 6, 4, sources_two) for g in EARLY]

    def forward_far(layer, relays, sources, between):
        copies = []
        for first, then in zip(FIRSTS, between):
            arrived(relays[first])
            for g in (first, first + 1):
                pack_far(layer, g)
                if g > 0:
                    copies.append(send_share(g, 10, 6, sources))
            then()
        return copies

    def keep_own(sources, i):
        copy = pltpu.make_async_copy(
            share.at[pl.ds(0, SHARE)], sources.at[pl.ds(NB, SHARE)], local_sem.at[i]
        )
        copy.start()
        copy.wait()

    def multiply(sources):
        def tile(e):
            return adjacency[jnp.clip(e & 255, 0, TILES)]

        def origin(e):
            return sources[jnp.clip(e >> 8, 0, NB + GROUPS * SHARE - 1)]

        def some(step, total):
            for i in range(UNROLL):
                pair = step * UNROLL + i
                one, two = order[0, 2 * pair], order[0, 2 * pair + 1]
                product = jnp.dot(
                    jnp.concatenate([tile(one), tile(two)], axis=1),
                    jnp.concatenate([origin(one), origin(two)], axis=0),
                    preferred_element_type=jnp.float32,
                )
                total = total * keep[0, pair] + product
                sums[pair] = total
            return total

        lax.fori_loop(0, PAIRS // UNROLL, some, jnp.zeros((BLOCK, BLOCK), jnp.float32))

    def summed(b):
        return sums[jnp.clip(order[1, b], 0, PAIRS - 1)] * keep[1, b]

    def nothing():
        pass

    others = range(1, GROUPS)

    pack_share([(0, table_one), (1, up_one), (2, down_one)])
    past = []

    def start_past():
        past.append(along_both(table_past, table_past, up_past, down_past, quarters[len(past)]))

    arrived(next_hop[0])
    start_past()
    arrived(next_hop[1])
    relays = {}
    for first in FIRSTS:
        pack_relay(up_two, down_two, first)
        relays[first] = send_relay(0, first)
    pack_share([(3, up_two), (4, down_two)])
    halo_copies = [send_share(g, 0, 10, sources_one) for g in others]

    def start_two():
        start_past()
        start_past()

    halo_copies += forward_far(
        0, relays, sources_one, (nothing, start_past, start_two, nothing)
    )
    hop = []
    for i in range(2):
        arrived(past[2 * i] + past[2 * i + 1])
        if i == 1:
            early = send_early()
        hop.append(along_both(up_past, down_past, up_past_two, down_past_two, halves[i]))
    keep_own(sources_one, 3)
    arrived(halo_copies)
    for copy in halo_copies:
        copy.wait_send()
    to_near.wait()
    to_sources.wait()
    multiply(sources_one)

    @pl.loop(0, NB)
    def _(b):
        hidden[b] = jnp.maximum(summed(b) + bias_one[...], 0.0).astype(jnp.bfloat16)

    hidden_out = pltpu.make_async_copy(hidden, hidden_at, local_sem.at[15])
    hidden_out.start()
    low, high = piece(0, 2), piece(1, 2)
    from_below = [send(hidden.at[low], near_y.at[0, low], at_y(1))]
    from_above = [send(hidden.at[high], near_y.at[1, high], at_y(-1))]
    from_below.append(send(hidden.at[high], near_y.at[0, high], at_y(1)))
    from_above.append(send(hidden.at[low], near_y.at[1, low], at_y(-1)))

    pack_share([(0, table_past), (1, up_past), (2, down_past)])
    last_copies = [send_share(g, 0, 6, sources_two) for g in others]
    last_copies += forward_early(early)
    for copies in relays.values():
        for copy in copies:
            copy.wait_send()
    arrived([from_below[0], from_above[0]])
    across = [
        send(near_y.at[0, low], far_y.at[low], at_y(1)),
        send(near_y.at[1, high], far_y.at[high], at_y(-1)),
    ]
    for copies in hop:
        arrived(copies)
    relays_two = {}
    for first in FIRSTS:
        pack_relay(up_past_two, down_past_two, first)
        relays_two[first] = send_relay(1, first)
        if first == EARLY[0]:
            continue
        pack_share([(3, up_past_two), (4, down_past_two)], first)
        for g in (first, first + 1):
            if g > 0:
                last_copies.append(send_share(g, 6, 4, sources_two))

    def part(shift):
        return weight[pl.ds(pl.multiple_of(lax.rem(y + shift, NY) * BLOCK, BLOCK), BLOCK), :]

    def project_hidden():
        arrived([from_below[1], from_above[1], *across])

        @pl.loop(0, NB // 4)
        def _(i):
            here = pl.ds(i * 4, 4)
            total = jnp.zeros((4 * BLOCK, BLOCK), jnp.float32)
            for rows, shift in ((hidden, 0), (near_y.at[0], 3), (near_y.at[1], 1), (far_y, 2)):
                total += jnp.dot(
                    rows[here].reshape(4 * BLOCK, BLOCK),
                    part(shift),
                    preferred_element_type=jnp.float32,
                )
            sources_two[here] = total.astype(jnp.bfloat16).reshape(4, BLOCK, BLOCK)

    last_copies += forward_far(1, relays_two, sources_two, (nothing, nothing, project_hidden, nothing))
    keep_own(sources_two, 4)
    arrived(last_copies)
    multiply(sources_two)

    outs = []
    for i in range(4):

        @pl.loop(i * NB // 4, (i + 1) * NB // 4)
        def _(b):
            embedding[b] = (summed(b) + bias_two[...]).astype(jnp.bfloat16)

        outs.append(
            pltpu.make_async_copy(embedding.at[quarters[i]], embedding_at.at[quarters[i]], local_sem.at[24 + i])
        )
        outs[i].start()
    hidden_out.wait()
    for copy in outs:
        copy.wait()
    assert used[0] == COPIES
    waited = halo_copies + [c for copies in relays.values() for c in copies]
    for copy in started:
        if not any(copy is w for w in waited):
            copy.wait_send()


def exchange(count, owner, block, target, source, bias_one, bias_two, weight_one, weight_two, features, history, adjacency):
    def blocks(*count):
        return pltpu.VMEM((*count, BLOCK, BLOCK), jnp.bfloat16)

    return pl.pallas_call(
        exchange_kernel,
        out_shape=(jax.ShapeDtypeStruct((NB, BLOCK, BLOCK), jnp.bfloat16),) * 2,
        in_specs=[SMEM] + [ANY] * 11,
        out_specs=(ANY, ANY),
        scratch_shapes=[
            pltpu.VMEM((1, HALO), jnp.int32),
            pltpu.VMEM((1, HALO), jnp.int32),
            pltpu.VMEM((1, TILES), jnp.int32),
            pltpu.VMEM((1, TILES), jnp.int32),
            pltpu.VMEM((1, BLOCK), jnp.float32),
            pltpu.VMEM((1, BLOCK), jnp.float32),
            pltpu.VMEM((4 * BLOCK, BLOCK), jnp.bfloat16),
            pltpu.VMEM((4 * BLOCK, BLOCK), jnp.bfloat16),
            blocks(NB),
            blocks(NB),
            pltpu.VMEM((8, 128), jnp.int32),
            pltpu.VMEM((8, 256), jnp.int32),
            pltpu.VMEM((8, 256), jnp.float32),
            pltpu.SMEM((8, 256), jnp.int32),
            pltpu.SMEM((8, 256), jnp.float32),
            pltpu.VMEM((5, GROUPS, 8, 128), jnp.int32),
            pltpu.SMEM((5, GROUPS, 8, 128), jnp.int32),
            pltpu.VMEM((2, NB * BLOCK // 4, 4 * BLOCK), jnp.bfloat16),
            *[blocks(NB)] * 10,
            blocks(2, 4),
            blocks(2, 4),
            blocks(4, 2 * GROUPS),
            blocks(2, 4, 2 * GROUPS),
            blocks(GROUPS * SHARE),
            blocks(NB + GROUPS * SHARE),
            blocks(NB + GROUPS * SHARE),
            blocks(TILES + 1),
            pltpu.VMEM((PAIRS, BLOCK, BLOCK), jnp.float32),
            blocks(2, NB),
            blocks(NB),
            pltpu.SemaphoreType.DMA((COPIES,)),
            pltpu.SemaphoreType.DMA((COPIES,)),
            pltpu.SemaphoreType.DMA((28,)),
        ],
        compiler_params=pltpu.CompilerParams(
            vmem_limit_bytes=60 * 2**20, collective_id=0, has_side_effects=True
        ),
        cost_estimate=pl.CostEstimate(
            flops=2 * 1024 * BLOCK**3, bytes_accessed=32 << 20, transcendentals=0
        ),
        name="exchange",
    )(
        count,
        owner,
        block,
        target,
        source,
        bias_one.reshape(1, BLOCK),
        bias_two.reshape(1, BLOCK),
        weight_one,
        weight_two,
        features,
        history,
        adjacency,
    )


def finish_kernel(hidden_at, embedding_at, hidden, embedding, held, sem):
    ins, outs = [], []
    for i, (at, to) in enumerate(((hidden_at, hidden), (embedding_at, embedding))):
        for j in range(2):
            part = pl.ds(j * (NB // 2), NB // 2)
            n = 2 * i + j
            ins.append(pltpu.make_async_copy(at.at[part], held.at[n], sem.at[n]))
            outs.append(pltpu.make_async_copy(held.at[n], to.at[part], sem.at[4 + n]))
    for copy in ins:
        copy.start()
    for come, go in zip(ins, outs):
        come.wait()
        go.start()
    for copy in outs:
        copy.wait()


def finish(hidden, embedding):
    table = jax.ShapeDtypeStruct((NB, BLOCK, BLOCK), jnp.bfloat16)
    return pl.pallas_call(
        finish_kernel,
        out_shape=(table, table),
        in_specs=[ANY] * 2,
        out_specs=(ANY, ANY),
        scratch_shapes=[
            pltpu.VMEM((4, NB // 2, BLOCK, BLOCK), jnp.bfloat16),
            pltpu.SemaphoreType.DMA((8,)),
        ],
        compiler_params=pltpu.CompilerParams(vmem_limit_bytes=60 * 2**20),
        cost_estimate=pl.CostEstimate(flops=0, bytes_accessed=4 << 20, transcendentals=0),
        name="finish",
    )(hidden, embedding)


def local(
    features,
    history,
    weight_one,
    weight_two,
    bias_one,
    bias_two,
    adjacency,
    halo_owner,
    halo_block,
    tile_target,
    tile_source,
    tile_count,
):
    hidden, embedding = exchange(
        tile_count,
        halo_owner,
        halo_block,
        tile_target,
        tile_source,
        bias_one,
        bias_two,
        weight_one,
        weight_two,
        features,
        history,
        adjacency,
    )
    hidden, embedding = finish(hidden, embedding)
    return (
        hidden.reshape(NB * BLOCK, BLOCK),
        embedding.reshape(NB * BLOCK, BLOCK),
    )


def solution(mesh):
    return jax.shard_map(
        local,
        mesh=mesh,
        in_specs=(
            P("row", None),
            P("row", None),
            P(None, "col"),
            P(None, "col"),
            P("col"),
            P("col"),
            P("row", None, None),
            P("row", None),
            P("row", None),
            P("row", None),
            P("row", None),
            P("row"),
        ),
        out_specs=(P("row", "col"), P("row", "col")),
        check_vma=False,
    )
```

```python
import jax
import jax.numpy as jnp
from jax import lax
from jax.experimental import pallas as pl
from jax.experimental.pallas import tpu as pltpu
from jax.sharding import PartitionSpec as P

BLOCK = 128
NB = 32
TILES = 192
HALO = 96
NX, NZ, NY = 4, 8, 4
GROUPS = 8
SHARE = 16
PAIRS = (TILES + NB) // 2
UNROLL = 8
FIRSTS = (4, 2, 6, 0)
MESH = pl.DeviceIdType.MESH

STEPS = (0, 7, 1, 6, 2, 5, 3, 4)

SMEM = pl.BlockSpec(memory_space=pltpu.SMEM)
VMEM = pl.BlockSpec(memory_space=pltpu.VMEM)
ANY = pl.BlockSpec(memory_space=pl.ANY)


def row_of(x, z, k):
    return x * (NZ * 2) + z * 2 + k


def member(x, k, group):
    dx, dk = group // 2, group % 2
    return lax.rem(x + dx, NX), k + dk - 2 * k * dk


def lane(shape, axis):
    return lax.broadcasted_iota(jnp.int32, shape, axis)


def upright(row):
    n = row.shape[1]
    shape = (n, n)
    diagonal = lane(shape, 0) == lane(shape, 1)
    return jnp.sum(jnp.where(diagonal, row, 0), axis=1, keepdims=True)


def request(x, z, k, owner, block, mine):
    row = owner[...]
    named = upright(row)
    square = (HALO, HALO)
    earlier = lane(square, 1) < lane(square, 0)
    nth = jnp.sum(jnp.where((row == named) & earlier, 1, 0), axis=1, keepdims=True)
    code = jnp.where(named >= 0, 2 * named + nth, -1)
    slots = lane((HALO, 128), 1)
    wanted = jnp.sum(jnp.where(code == slots, upright(block[...]), 0), axis=0, keepdims=True)
    mine[...] = jnp.broadcast_to(wanted, (8, 128))
    o = jnp.maximum(named, 0)
    ox, oz, ok = o >> 4, (o >> 1) & 7, o & 1
    group = ((x - ox) & 3) * 2 + (k + ok - 2 * k * ok)
    step = (oz - z) & 7
    spot = jnp.zeros_like(o)
    for i, s in enumerate(STEPS):
        spot = jnp.where(step == s, 2 * i, spot)
    return group * SHARE + spot + jnp.minimum(nth, 1)


def sort(live, target, source, place, listed, kept):
    ids = lane((1, TILES), 1)
    s = source[...]
    slots = lane((HALO, TILES), 0)
    halo = jnp.sum(jnp.where(slots == s - NB, place, 0), axis=0, keepdims=True)
    at = jnp.where(s < NB, s, halo + NB)
    entry = upright(ids + 256 * at)
    row = jnp.where(ids < live, target[...], NB)
    goal = upright(row)
    key = row * 256 + ids
    rank = jnp.sum(jnp.where(key < upright(key), 1, 0), axis=1, keepdims=True)
    before = jnp.sum(jnp.where(row < goal, 1, 0), axis=1, keepdims=True)
    mine = goal == lane((TILES, 128), 1)
    many = jnp.sum(jnp.where(mine, 1, 0), axis=0, keepdims=True)
    pairs = (many + 1) >> 1
    square = (128, 128)
    start = jnp.sum(
        jnp.where(lane(square, 0) < lane(square, 1), upright(pairs), 0), axis=0, keepdims=True
    )
    spot = 2 * jnp.sum(jnp.where(mine, start, 0), axis=1, keepdims=True) + rank - before
    here = spot == lane((TILES, 256), 1)
    filled = jnp.sum(jnp.where(here, 1, 0), axis=0, keepdims=True)
    order = jnp.sum(jnp.where(here, entry, 0), axis=0, keepdims=True)
    listed[0:1, 0:256] = jnp.where(filled > 0, order, TILES)
    opens = (upright(start) == lane(square, 1)) & (upright(many) > 0)
    first = jnp.sum(jnp.where(opens, 1, 0), axis=0, keepdims=True)
    kept[0:1, 0:128] = jnp.where(first > 0, 0.0, 1.0)
    listed[1:2, 0:128] = jnp.maximum(start + pairs - 1, 0)
    kept[1:2, 0:128] = jnp.where(many > 0, 1.0, 0.0)


COPIES = 71


def exchange_kernel(
    count,
    owner_at,
    block_at,
    target_at,
    source_at,
    bias_one_at,
    bias_two_at,
    first_weight_at,
    weight_at,
    features,
    history,
    adjacency_at,
    hidden_at,
    embedding_at,
    owner,
    block,
    target,
    source,
    bias_one,
    bias_two,
    first_weight,
    weight,
    hidden,
    embedding,
    mine,
    listed,
    kept,
    order,
    keep,
    wanted_all,
    wanted,
    stage,
    table_one,
    table_past,
    up_one,
    down_one,
    up_two,
    down_two,
    up_past,
    down_past,
    up_past_two,
    down_past_two,
    relay_out,
    relay_in,
    share,
    sources_one,
    sources_two,
    adjacency,
    sums,
    near_y,
    far_y,
    send_sem,
    recv_sem,
    local_sem,
):
    row = lax.axis_index("row")
    y = lax.axis_index("col")
    x, z, k = row // 16, lax.rem(row // 2, NZ), lax.rem(row, 2)
    me = x * 2 + k
    used = [0]

    def at_z(step):
        return (row_of(x, lax.rem(z + step + NZ, NZ), k), y)

    def at_slab(group):
        ox, ok = member(x, k, group)
        return (row_of(ox, z, ok), y)

    def at_y(step):
        return (row, lax.rem(y + step + NY, NY))

    peers = [at_z(s) for s in (1, -1, 2, -2)]
    peers += [at_slab(g) for g in range(1, GROUPS)]
    peers += [at_y(s) for s in (1, -1)]

    barrier = pltpu.get_barrier_semaphore()
    for peer in peers:
        pl.semaphore_signal(barrier, inc=1, device_id=peer, device_id_type=MESH)

    small = [
        pltpu.make_async_copy(at, here, local_sem.at[16 + i])
        for i, (at, here) in enumerate(
            (
                (first_weight_at, first_weight),
                (owner_at, owner),
                (block_at, block),
                (target_at, target),
                (source_at, source),
                (bias_one_at, bias_one),
                (bias_two_at, bias_two),
                (weight_at, weight),
            )
        )
    ]
    for copy in small[:3]:
        copy.start()

    rows = NB * BLOCK // 4
    pieces = [(table, w, at, i) for table, w, at in ((table_one, first_weight, features), (table_past, weight, history)) for i in range(4)]
    fetches = [
        pltpu.make_async_copy(at.at[pl.ds(i * rows, rows)], stage.at[n % 2], local_sem.at[5 + n])
        for n, (_, _, at, i) in enumerate(pieces)
    ]

    def project(n):
        table, w, _, i = pieces[n]
        fetches[n].wait()

        @pl.loop(0, NB // 8)
        def _(j):
            part = stage[n % 2, pl.ds(j * 2 * BLOCK, 2 * BLOCK)]
            product = jnp.dot(part, w[...], preferred_element_type=jnp.float32)
            table[pl.ds(i * (NB // 4) + 2 * j, 2)] = product.astype(jnp.bfloat16).reshape(2, BLOCK, BLOCK)

        if n + 2 < len(pieces):
            fetches[n + 2].start()

    fetches[0].start()
    fetches[1].start()
    for copy in small[3:]:
        copy.start()
    to_near = pltpu.make_async_copy(adjacency_at, adjacency.at[pl.ds(0, TILES)], local_sem.at[0])
    to_near.start()
    adjacency[TILES] = jnp.zeros((BLOCK, BLOCK), jnp.bfloat16)
    for copy in small:
        copy.wait()
    place = request(x, z, k, owner, block, mine)
    project(0)
    pl.semaphore_wait(barrier, len(peers))

    started = []

    def send(src, dst, device, shared=None):
        i = used[0] if shared is None else shared
        used[0] += shared is None
        copy = pltpu.make_async_remote_copy(
            src_ref=src,
            dst_ref=dst,
            send_sem=send_sem.at[i],
            recv_sem=recv_sem.at[i],
            device_id=device,
            device_id_type=MESH,
        )
        copy.start()
        if shared is None:
            started.append(copy)
        return copy

    def arrived(copies):
        for copy in copies:
            copy.wait_recv()

    def piece(i, count):
        return pl.ds(i * (NB // count), NB // count)

    def along_both(up_from, down_from, up_to, down_to, p):
        return [send(up_from.at[p], up_to.at[p], at_z(1)), send(down_from.at[p], down_to.at[p], at_z(-1))]

    quarters = [piece(i, 4) for i in range(4)]
    halves = [piece(i, 2) for i in range(2)]
    hop = [along_both(table_one, table_one, up_one, down_one, quarters[0])]
    asks = [send(mine, wanted_all.at[2, me], at_slab(g)) for g in range(1, GROUPS)]
    wanted_all[2, me] = mine[...]
    project(1)
    hop.append(along_both(table_one, table_one, up_one, down_one, quarters[1]))
    arrived(asks)
    asks = [send(wanted_all.at[2], wanted_all.at[2 - s], at_z(s)) for s in (1, -1, 2, -2)]
    project(2)
    project(3)
    hop.append(along_both(table_one, table_one, up_one, down_one, halves[1]))
    to_sources = pltpu.make_async_copy(table_one, sources_one.at[pl.ds(0, NB)], local_sem.at[1])
    to_sources.start()
    sort(count[0], target, source, place, listed, kept)
    to_order = pltpu.make_async_copy(listed, order, local_sem.at[13])
    to_order.start()
    to_keep = pltpu.make_async_copy(kept, keep, local_sem.at[14])
    to_keep.start()
    for i in range(4):
        project(4 + i)
    next_hop = []
    for i in range(2):
        arrived(hop[i])
    next_hop.append(along_both(up_one, down_one, up_two, down_two, halves[0]))
    arrived(asks)
    to_scalars = pltpu.make_async_copy(wanted_all, wanted, local_sem.at[2])
    to_scalars.start()
    to_scalars.wait()
    to_order.wait()
    to_keep.wait()
    arrived(hop[2])
    next_hop.append(along_both(up_one, down_one, up_two, down_two, halves[1]))

    def pick(shift, group, step, slot):
        ox, ok = member(x, k, group)
        o = row_of(x, lax.rem(z + step + NZ, NZ), k)
        return jnp.clip(wanted[2 + shift, ox * 2 + ok, 0, 2 * o + slot], 0, NB - 1)

    def pack_share(parts, first=None):
        @pl.loop(0 if first is None else first, GROUPS if first is None else first + 2)
        def _(g):
            for i, table in parts:
                for slot in range(2):
                    share[g * SHARE + 2 * i + slot] = table[pick(0, g, STEPS[i], slot)]

    def send_share(g, start, size, sources):
        at = g * SHARE + start
        layer = 0 if sources is sources_one else 1
        send(share.at[pl.ds(at, size)], sources.at[pl.ds(NB + at, size)], at_slab(g), COPIES + layer)

    def shares(layer, sources):
        rest = (GROUPS - 1) * SHARE
        return pltpu.make_async_remote_copy(
            src_ref=share.at[pl.ds(SHARE, rest)],
            dst_ref=sources.at[pl.ds(NB + SHARE, rest)],
            send_sem=send_sem.at[COPIES + layer],
            recv_sem=recv_sem.at[COPIES + layer],
            device_id=at_slab(1),
            device_id_type=MESH,
        )

    def pack_relay(up, down, first):
        @pl.loop(first, first + 2)
        def _(g):
            for side, (table, sign) in enumerate(((up, 1), (down, -1))):
                for slot in range(2):
                    relay_out[side, g * 2 + slot] = table[pick(sign, g, -2 * sign, slot)]
                relay_out[2 + side, g] = table[pick(2 * sign, g, -2 * sign, side)]

    def send_relay(layer, first):
        near, far = pl.ds(first * 2, 4), pl.ds(first, 2)
        copies = []
        for side, sign in ((0, 1), (1, -1)):
            copies.append(send(relay_out.at[2 + side, far], relay_in.at[layer, 2 + side, far], at_z(2 * sign)))
            copies.append(send(relay_out.at[side, near], relay_in.at[layer, side, near], at_z(sign)))
        return copies

    def pack_far(layer, g):
        at = g * SHARE
        share[at + 10] = relay_in[layer, 0, 2 * g]
        share[at + 11] = relay_in[layer, 0, 2 * g + 1]
        share[at + 12] = relay_in[layer, 1, 2 * g]
        share[at + 13] = relay_in[layer, 1, 2 * g + 1]
        share[at + 14] = relay_in[layer, 2, g]
        share[at + 15] = relay_in[layer, 3, g]

    def forward_far(layer, relays, sources, between):
        for first, then in zip(FIRSTS, between):
            arrived(relays[first])
            for g in (first, first + 1):
                pack_far(layer, g)
                if g > 0:
                    send_share(g, 10, 6, sources)
            then()

    def keep_own(sources, i):
        copy = pltpu.make_async_copy(
            share.at[pl.ds(0, SHARE)], sources.at[pl.ds(NB, SHARE)], local_sem.at[i]
        )
        copy.start()
        copy.wait()

    def multiply(sources):
        def tile(e):
            return adjacency[jnp.clip(e & 255, 0, TILES)]

        def origin(e):
            return sources[jnp.clip(e >> 8, 0, NB + GROUPS * SHARE - 1)]

        def some(step, total):
            for i in range(UNROLL):
                pair = step * UNROLL + i
                one, two = order[0, 2 * pair], order[0, 2 * pair + 1]
                product = jnp.dot(
                    jnp.concatenate([tile(one), tile(two)], axis=1),
                    jnp.concatenate([origin(one), origin(two)], axis=0),
                    preferred_element_type=jnp.float32,
                )
                total = total * keep[0, pair] + product
                sums[pair] = total
            return total

        lax.fori_loop(0, PAIRS // UNROLL, some, jnp.zeros((BLOCK, BLOCK), jnp.float32))

    def summed(b):
        return sums[jnp.clip(order[1, b], 0, PAIRS - 1)] * keep[1, b]

    def nothing():
        pass

    others = range(1, GROUPS)

    pack_share([(0, table_one), (1, up_one), (2, down_one)])
    past = []

    def start_past():
        past.append(along_both(table_past, table_past, up_past, down_past, quarters[len(past)]))

    arrived(next_hop[0])
    start_past()
    arrived(next_hop[1])
    relays = {}
    for first in FIRSTS:
        pack_relay(up_two, down_two, first)
        relays[first] = send_relay(0, first)
    pack_share([(3, up_two), (4, down_two)])
    for g in others:
        send_share(g, 0, 10, sources_one)

    def start_two():
        start_past()
        start_past()

    forward_far(
        0, relays, sources_one, (nothing, start_past, start_two, nothing)
    )
    hop = []
    for i in range(2):
        arrived(past[2 * i] + past[2 * i + 1])
        hop.append(along_both(up_past, down_past, up_past_two, down_past_two, halves[i]))
    keep_own(sources_one, 3)
    shares(0, sources_one).wait_recv()
    shares(0, sources_one).wait_send()
    pack_share([(0, table_past), (1, up_past), (2, down_past)])
    for g in others:
        send_share(g, 0, 6, sources_two)
    to_near.wait()
    to_sources.wait()
    multiply(sources_one)

    @pl.loop(0, NB)
    def _(b):
        hidden[b] = jnp.maximum(summed(b) + bias_one[...], 0.0).astype(jnp.bfloat16)

    hidden_out = pltpu.make_async_copy(hidden, hidden_at, local_sem.at[15])
    hidden_out.start()
    low, high = piece(0, 2), piece(1, 2)
    from_below = [send(hidden.at[low], near_y.at[0, low], at_y(1))]
    from_above = [send(hidden.at[high], near_y.at[1, high], at_y(-1))]
    from_below.append(send(hidden.at[high], near_y.at[0, high], at_y(1)))
    from_above.append(send(hidden.at[low], near_y.at[1, low], at_y(-1)))

    for copies in relays.values():
        for copy in copies:
            copy.wait_send()
    arrived([from_below[0], from_above[0]])
    across = [
        send(near_y.at[0, low], far_y.at[low], at_y(1)),
        send(near_y.at[1, high], far_y.at[high], at_y(-1)),
    ]
    for copies in hop:
        arrived(copies)
    relays_two = {}
    for first in FIRSTS:
        pack_relay(up_past_two, down_past_two, first)
        relays_two[first] = send_relay(1, first)
        pack_share([(3, up_past_two), (4, down_past_two)], first)
        for g in (first, first + 1):
            if g > 0:
                send_share(g, 6, 4, sources_two)

    def part(shift):
        return weight[pl.ds(pl.multiple_of(lax.rem(y + shift, NY) * BLOCK, BLOCK), BLOCK), :]

    def project_hidden():
        arrived([from_below[1], from_above[1], *across])

        @pl.loop(0, NB // 4)
        def _(i):
            here = pl.ds(i * 4, 4)
            total = jnp.zeros((4 * BLOCK, BLOCK), jnp.float32)
            for rows, shift in ((hidden, 0), (near_y.at[0], 3), (near_y.at[1], 1), (far_y, 2)):
                total += jnp.dot(
                    rows[here].reshape(4 * BLOCK, BLOCK),
                    part(shift),
                    preferred_element_type=jnp.float32,
                )
            sources_two[here] = total.astype(jnp.bfloat16).reshape(4, BLOCK, BLOCK)

    forward_far(1, relays_two, sources_two, (nothing, nothing, project_hidden, nothing))
    keep_own(sources_two, 4)
    shares(1, sources_two).wait_recv()
    multiply(sources_two)

    outs = []
    for i in range(4):

        @pl.loop(i * NB // 4, (i + 1) * NB // 4)
        def _(b):
            embedding[b] = (summed(b) + bias_two[...]).astype(jnp.bfloat16)

        outs.append(
            pltpu.make_async_copy(embedding.at[quarters[i]], embedding_at.at[quarters[i]], local_sem.at[24 + i])
        )
        outs[i].start()
    hidden_out.wait()
    for copy in outs:
        copy.wait()
    assert used[0] == COPIES
    shares(1, sources_two).wait_send()
    waited = [c for copies in relays.values() for c in copies]
    for copy in started:
        if not any(copy is w for w in waited):
            copy.wait_send()


def exchange(count, owner, block, target, source, bias_one, bias_two, weight_one, weight_two, features, history, adjacency):
    def blocks(*count):
        return pltpu.VMEM((*count, BLOCK, BLOCK), jnp.bfloat16)

    return pl.pallas_call(
        exchange_kernel,
        out_shape=(jax.ShapeDtypeStruct((NB, BLOCK, BLOCK), jnp.bfloat16),) * 2,
        in_specs=[SMEM] + [ANY] * 11,
        out_specs=(ANY, ANY),
        scratch_shapes=[
            pltpu.VMEM((1, HALO), jnp.int32),
            pltpu.VMEM((1, HALO), jnp.int32),
            pltpu.VMEM((1, TILES), jnp.int32),
            pltpu.VMEM((1, TILES), jnp.int32),
            pltpu.VMEM((1, BLOCK), jnp.float32),
            pltpu.VMEM((1, BLOCK), jnp.float32),
            pltpu.VMEM((4 * BLOCK, BLOCK), jnp.bfloat16),
            pltpu.VMEM((4 * BLOCK, BLOCK), jnp.bfloat16),
            blocks(NB),
            blocks(NB),
            pltpu.VMEM((8, 128), jnp.int32),
            pltpu.VMEM((8, 256), jnp.int32),
            pltpu.VMEM((8, 256), jnp.float32),
            pltpu.SMEM((8, 256), jnp.int32),
            pltpu.SMEM((8, 256), jnp.float32),
            pltpu.VMEM((5, GROUPS, 8, 128), jnp.int32),
            pltpu.SMEM((5, GROUPS, 8, 128), jnp.int32),
            pltpu.VMEM((2, NB * BLOCK // 4, 4 * BLOCK), jnp.bfloat16),
            *[blocks(NB)] * 10,
            blocks(4, 2 * GROUPS),
            blocks(2, 4, 2 * GROUPS),
            blocks(GROUPS * SHARE),
            blocks(NB + GROUPS * SHARE),
            blocks(NB + GROUPS * SHARE),
            blocks(TILES + 1),
            pltpu.VMEM((PAIRS, BLOCK, BLOCK), jnp.float32),
            blocks(2, NB),
            blocks(NB),
            pltpu.SemaphoreType.DMA((COPIES + 2,)),
            pltpu.SemaphoreType.DMA((COPIES + 2,)),
            pltpu.SemaphoreType.DMA((28,)),
        ],
        compiler_params=pltpu.CompilerParams(
            vmem_limit_bytes=60 * 2**20, collective_id=0, has_side_effects=True
        ),
        cost_estimate=pl.CostEstimate(
            flops=2 * 1024 * BLOCK**3, bytes_accessed=32 << 20, transcendentals=0
        ),
        name="exchange",
    )(
        count,
        owner,
        block,
        target,
        source,
        bias_one.reshape(1, BLOCK),
        bias_two.reshape(1, BLOCK),
        weight_one,
        weight_two,
        features,
        history,
        adjacency,
    )


def finish_kernel(hidden_at, embedding_at, hidden, embedding, held, sem):
    ins, outs = [], []
    for i, (at, to) in enumerate(((hidden_at, hidden), (embedding_at, embedding))):
        for j in range(2):
            part = pl.ds(j * (NB // 2), NB // 2)
            n = 2 * i + j
            ins.append(pltpu.make_async_copy(at.at[part], held.at[n], sem.at[n]))
            outs.append(pltpu.make_async_copy(held.at[n], to.at[part], sem.at[4 + n]))
    for copy in ins:
        copy.start()
    for come, go in zip(ins, outs):
        come.wait()
        go.start()
    for copy in outs:
        copy.wait()


def finish(hidden, embedding):
    table = jax.ShapeDtypeStruct((NB, BLOCK, BLOCK), jnp.bfloat16)
    return pl.pallas_call(
        finish_kernel,
        out_shape=(table, table),
        in_specs=[ANY] * 2,
        out_specs=(ANY, ANY),
        scratch_shapes=[
            pltpu.VMEM((4, NB // 2, BLOCK, BLOCK), jnp.bfloat16),
            pltpu.SemaphoreType.DMA((8,)),
        ],
        compiler_params=pltpu.CompilerParams(vmem_limit_bytes=60 * 2**20),
        cost_estimate=pl.CostEstimate(flops=0, bytes_accessed=4 << 20, transcendentals=0),
        name="finish",
    )(hidden, embedding)


def local(
    features,
    history,
    weight_one,
    weight_two,
    bias_one,
    bias_two,
    adjacency,
    halo_owner,
    halo_block,
    tile_target,
    tile_source,
    tile_count,
):
    hidden, embedding = exchange(
        tile_count,
        halo_owner,
        halo_block,
        tile_target,
        tile_source,
        bias_one,
        bias_two,
        weight_one,
        weight_two,
        features,
        history,
        adjacency,
    )
    hidden, embedding = finish(hidden, embedding)
    return (
        hidden.reshape(NB * BLOCK, BLOCK),
        embedding.reshape(NB * BLOCK, BLOCK),
    )


def solution(mesh):
    return jax.shard_map(
        local,
        mesh=mesh,
        in_specs=(
            P("row", None),
            P("row", None),
            P(None, "col"),
            P(None, "col"),
            P("col"),
            P("col"),
            P("row", None, None),
            P("row", None),
            P("row", None),
            P("row", None),
            P("row", None),
            P("row"),
        ),
        out_specs=(P("row", "col"), P("row", "col")),
        check_vma=False,
    )
```
